32 devices in a mesh: groups: 2 (over y), ctx: 4 (over z), head: 2 (over x), sub: 2 (over core).
Axes of the slice: x: 2, y: 2, z: 4, core: 2. Of those that a mesh axis runs over, the one named last changes fastest.
Arguments:
- queries: bfloat16 [4096, 4096], P(('groups', 'ctx'), ('head', 'sub')), parts along dimension 0, may hold values from -6 to 6
- keys: bfloat16 [4096, 2, 4096], P(('groups', 'ctx'), None, ('head', 'sub')), parts along dimension 0, may hold values from -6 to 6
- values: bfloat16 [4096, 2, 4096], P(('groups', 'ctx'), None, ('head', 'sub')), parts along dimension 0, may hold values from -0.59765625 to 0.59765625
- betas: float32 [4096, 2, 32], P(('groups', 'ctx'), None, ('head', 'sub')), parts along dimension 0, may hold values from 0.3 to 2
- log_decay: float32 [4096, 32], P(('groups', 'ctx'), ('head', 'sub')), parts along dimension 0, may hold values from -1.5 to 0, as said below
- attn_queries: bfloat16 [4096, 4096], P(('groups', 'ctx'), ('head', 'sub')), parts along dimension 0, may hold values from -24 to 24
- attn_keys: bfloat16 [4096, 4096], P(('groups', 'ctx'), ('head', 'sub')), parts along dimension 0, may hold values from -24 to 24
Outputs:
- retained: bfloat16 [4096, 4096], P(('groups', 'ctx'), ('head', 'sub')), parts along dimension 0
- attended: bfloat16 [4096, 4096], P(('groups', 'ctx'), ('head', 'sub')), parts along dimension 0
The draws below stay inside these ranges and needn't reach their ends.
There are 2 independent parts, one for each index of `groups`. The reference program is written for one: setup_inputs(seed, part) draws one part's arguments, and reference() takes and returns one part's arrays. A program takes and returns all parts, laid end to end along the dimension named above; each array names one. Nothing has to cross between parts.
Inputs may be any that keep to these rules, and one draw needn't show every extreme that they name: `log_decay`: logarithms of decays; a few tokens of each head take sudden drops, which may fall on the same token.
All inputs are finite; a program needn't handle non-finite values.
Results may differ from the reference program's by a relative error of at most 0.0057.
Values may be sent and summed in bfloat16 or wider, within the bound.
No kernel may reach another device: no remote copies, remote signals or barrier semaphores. Data moves between devices by JAX's collectives and lax.ppermute only.
A program may use at most 128 MiB of HBM per device.

```python
import jax
import jax.numpy as jnp
from jax import lax

HEADS = 32
HD = 128
NREF = 2
SPAN = 32
TOK_DEV = 512
TOKENS = 2048


def slow_heads(key, share):
    return jax.random.bernoulli(jax.random.fold_in(key, 101), share, (HEADS,))


def draw_log_decay(key, part):
    share = 0.5
    slow = slow_heads(key, share)
    first, second, third, fourth, fifth = jax.random.split(jax.random.fold_in(key, 202), 5)
    fast_rate = jnp.exp(jax.random.uniform(first, (HEADS,), jnp.float32, jnp.log(1.0 / 50.0), jnp.log(1.0 / 30.0)))
    forgetting_speed = jnp.where(slow, 0.15 / TOKENS, fast_rate)
    blocks = TOKENS // TOK_DEV
    multiplier_coefficient = jnp.exp(jax.random.uniform(second, (blocks, 1, HEADS), jnp.float32, -0.7, 0.7))
    multiplier_coefficient = jnp.broadcast_to(multiplier_coefficient, (blocks, TOK_DEV, HEADS)).reshape(TOKENS, HEADS)
    approximate_guess = jax.random.uniform(fifth, (TOKENS, HEADS), jnp.float32, 0.5, 1.5)
    spots = jax.random.randint(third, (2, HEADS), 0, TOKENS)
    forgetting_amounts = jnp.log(jax.random.uniform(fourth, (2, HEADS), jnp.float32, 0.5, 0.8))
    contact_indicator = jnp.arange(TOKENS)[:, None, None] == spots[None, :, :]
    reflection_bundles = jnp.sum(jnp.where(contact_indicator, forgetting_amounts[None, :, :], 0.0), axis=1)
    return (-forgetting_speed[None, :] * multiplier_coefficient * approximate_guess + reflection_bundles).astype(jnp.float32)


def draw_betas(key, part):
    share = 0.5
    slow = slow_heads(key, share)
    first, second = jax.random.split(jax.random.fold_in(key, 303), 2)
    nearly = 2.0 - jax.random.uniform(first, (TOKENS, NREF, HEADS), jnp.float32, 0.0, 0.004)
    broad = jax.random.uniform(second, (TOKENS, NREF, HEADS), jnp.float32, 0.3, 1.9)
    return jnp.where(slow[None, None, :], nearly, broad).astype(jnp.float32)


def draw_attn_keys(key, part):
    base = jnp.clip(jax.random.normal(jax.random.fold_in(key, 505), (TOKENS, HEADS * HD), jnp.float32), -6.0, 6.0)
    return base.astype(jnp.bfloat16)


def draw_attn_queries(key, part):
    base = jnp.clip(jax.random.normal(jax.random.fold_in(key, 606), (TOKENS, HEADS * HD), jnp.float32), -6.0, 6.0)
    return base.astype(jnp.bfloat16)


def levels(rng, extent, shards, low, top_value):
    def one(axis_at, blocks):
        steps = jax.random.uniform(jax.random.fold_in(jax.random.fold_in(rng, 6), axis_at), (blocks,), jnp.float32, low / len(shards), top_value / len(shards))
        return jnp.repeat(jnp.exp(steps), extent[axis_at] // blocks).reshape((-1,) + (1,) * (len(extent) - axis_at - 1))

    gain = one(*shards[0])
    for cut in shards[1:]:
        gain = gain * one(*cut)
    return gain


def normal_values(key, extent, scale, reach, cuts=(), kind=jnp.bfloat16):
    level = levels(key, extent, cuts, -0.22, 0.18) if cuts else 1.0
    array = jax.random.normal(key, extent, jnp.float32) * scale * level
    return jnp.minimum(jnp.maximum(array, -reach), reach).astype(kind)


def setup_inputs(seed: int = 0, part: int = 0) -> dict:
    arg_keys = jax.random.split(jax.random.key(seed), 8)
    part_splits = jax.random.split(jax.random.fold_in(arg_keys[7], part), 8)
    return {
        "queries": normal_values(part_splits[0], (TOKENS, HEADS * HD), 1.0, 6.0, ((0, 4), (1, 4))),
        "keys": normal_values(part_splits[1], (TOKENS, NREF, HEADS * HD), 1.0, 6.0, ((0, 4), (2, 4))),
        "values": normal_values(part_splits[2], (TOKENS, NREF, HEADS * HD), 0.1, 0.59765625, ((0, 4), (2, 4))),
        "betas": draw_betas(jax.random.fold_in(jax.random.fold_in(arg_keys[7], part), 71), part),
        "log_decay": draw_log_decay(jax.random.fold_in(jax.random.fold_in(arg_keys[7], part), 71), part),
        "attn_queries": draw_attn_queries(jax.random.fold_in(jax.random.fold_in(arg_keys[7], part), 71), part),
        "attn_keys": draw_attn_keys(jax.random.fold_in(jax.random.fold_in(arg_keys[7], part), 71), part),
    }


highest = lax.Precision.HIGHEST

def unit_rows(matrix):
    return matrix * lax.rsqrt(lax.optimization_barrier(jnp.sum(matrix * matrix, axis=-1, keepdims=True)) + 1e-06)

def arrange(block_queries, block_keys, block_values, block_betas, segment_forgetting):
    count = block_queries.shape[0]
    heads = block_betas.shape[2]
    width = block_queries.shape[1] // heads
    query_heads = block_queries.reshape(count, heads, width).transpose(1, 0, 2).astype(jnp.float32)
    key_heads = block_keys.reshape(count, NREF, heads, width).transpose(2, 0, 1, 3).reshape(heads, count * NREF, width).astype(jnp.float32)
    value_heads = block_values.reshape(count, NREF, heads, width).transpose(2, 0, 1, 3).reshape(heads, count * NREF, width).astype(jnp.float32)
    beta_heads = block_betas.transpose(2, 0, 1).reshape(heads, count * NREF)
    stepped = jnp.concatenate([segment_forgetting[:, None, :], jnp.zeros((count, NREF - 1, heads), segment_forgetting.dtype)], axis=1)
    decay_heads = stepped.transpose(2, 0, 1).reshape(heads, count * NREF)
    return (unit_rows(query_heads), unit_rows(key_heads), value_heads, beta_heads, decay_heads)

def span_factors(key_rows, value_rows, beta_rows, decay_rows):
    size = key_rows.shape[0]
    width = key_rows.shape[1]
    level = jnp.cumsum(decay_rows)
    gram = jnp.dot(key_rows, key_rows.T, precision=highest)
    spread = jnp.minimum(level[:, None] - level[None, :], 0.0)
    below = jnp.arange(size)[:, None] > jnp.arange(size)[None, :]
    mixing = jnp.where(below, beta_rows[:, None] * jnp.exp(spread) * gram, 0.0) + jnp.eye(size, dtype=key_rows.dtype)
    sides = jnp.concatenate([beta_rows[:, None] * value_rows, (beta_rows * jnp.exp(level))[:, None] * key_rows], axis=1)
    solved = jax.scipy.linalg.solve_triangular(mixing, sides, lower=True, unit_diagonal=True)
    written = solved[:, :width]
    carried = solved[:, width:]
    trailing = jnp.exp(level[-1] - level)
    transition = jnp.exp(level[-1]) * jnp.eye(width, dtype=key_rows.dtype) - jnp.dot((trailing[:, None] * carried).T, key_rows, precision=highest)
    addition = jnp.dot((trailing[:, None] * written).T, key_rows, precision=highest)
    return (written, carried, level, transition, addition)

def span_outputs(state, query_rows, key_rows, written, carried, level):
    count = query_rows.shape[0]
    size = key_rows.shape[0]
    fresh = written - jnp.dot(carried, state.T, precision=highest)
    reached = level[NREF - 1::NREF]
    spread = jnp.minimum(reached[:, None] - level[None, :], 0.0)
    visible = jnp.arange(size)[None, :] <= NREF * jnp.arange(count)[:, None] + NREF - 1
    weights = jnp.where(visible, jnp.exp(spread) * jnp.dot(query_rows, key_rows.T, precision=highest), 0.0)
    return jnp.exp(reached)[:, None] * jnp.dot(query_rows, state.T, precision=highest) + jnp.dot(weights, fresh, precision=highest)

def head_span(state, query_rows, key_rows, value_rows, beta_rows, decay_rows):
    written, carried, level, transition, addition = span_factors(key_rows, value_rows, beta_rows, decay_rows)
    produced = span_outputs(state, query_rows, key_rows, written, carried, level)
    return (jnp.dot(state, transition, precision=highest) + addition, produced)

def block_attention(block_queries, block_keys, block_values, earlier_ok, heads):
    count = block_queries.shape[0]
    width = block_queries.shape[1] // heads
    query_heads = block_queries.reshape(count, heads, width).astype(jnp.float32)
    key_heads = block_keys.reshape(2 * count, heads, width).astype(jnp.float32)
    value_heads = block_values.reshape(2 * count, heads, width).astype(jnp.float32)
    attention_scores = jnp.einsum('qhd,khd->hqk', query_heads, key_heads) * width ** (-0.5)
    position = jnp.arange(2 * count)[None, :]
    ownrow = jnp.arange(count)[:, None]
    allowed = jnp.where(position >= count, position - count <= ownrow, earlier_ok)
    attention_scores = jnp.where(allowed[None], attention_scores, -1e+30)
    largest = lax.optimization_barrier(jnp.max(attention_scores, axis=2, keepdims=True))
    expanded = jnp.exp(attention_scores - largest)
    weights = (expanded / lax.optimization_barrier(jnp.sum(expanded, axis=2, keepdims=True))).astype(jnp.bfloat16)
    mixed = jnp.einsum('hqk,khd->qhd', weights.astype(jnp.float32), value_heads)
    return mixed.reshape(count, heads * width).astype(jnp.bfloat16)

def reference(queries, keys, values, betas, log_decay, attn_queries, attn_keys):
    heads = betas.shape[2]
    width = queries.shape[1] // heads
    blocks = queries.shape[0] // SPAN

    def advance(state, pieces):
        query_heads, key_heads, value_heads, beta_heads, decay_heads = arrange(*pieces)
        state, produced = jax.vmap(head_span)(state, query_heads, key_heads, value_heads, beta_heads, decay_heads)
        return (state, produced.transpose(1, 0, 2).reshape(SPAN, heads * width))
    pieces = (queries.reshape(blocks, SPAN, heads * width), keys.reshape(blocks, SPAN, NREF, heads * width), values.reshape(blocks, SPAN, NREF, heads * width), betas.reshape(blocks, SPAN, NREF, heads), log_decay.reshape(blocks, SPAN, heads))
    start = jnp.zeros((heads, width, width), jnp.float32)
    closing_memory_matrix, produced = lax.scan(advance, start, pieces)
    retained = produced.reshape(blocks * SPAN, heads * width).astype(jnp.bfloat16)
    padded_keys = jnp.concatenate([jnp.zeros((TOK_DEV, heads * width), jnp.bfloat16), attn_keys], axis=0)
    padded_values = jnp.concatenate([jnp.zeros((TOK_DEV, heads * width), jnp.bfloat16), retained], axis=0)

    def attend(index):
        begin = (index * TOK_DEV).astype(jnp.int32)
        block_queries = lax.dynamic_slice_in_dim(attn_queries, begin, TOK_DEV, 0)
        block_keys = lax.dynamic_slice_in_dim(padded_keys, begin, 2 * TOK_DEV, 0)
        block_values = lax.dynamic_slice_in_dim(padded_values, begin, 2 * TOK_DEV, 0)
        return block_attention(block_queries, block_keys, block_values, index > 0, heads)
    attended = lax.map(attend, jnp.arange(queries.shape[0] // TOK_DEV, dtype=jnp.int32))
    return (retained, attended.reshape(queries.shape[0], heads * width))
```

```python
import functools
import math

import jax
import jax.numpy as jnp
from jax import lax
from jax.experimental import pallas as pl
from jax.experimental.pallas import tpu as pltpu
from jax.sharding import PartitionSpec as P

f32=jnp.float32; bf16=jnp.bfloat16
def dot(a,b): return lax.dot_general(a,b,(((1,),(0,)),((),())),preferred_element_type=f32)
def dot_nt(a,b): return lax.dot_general(a,b,(((1,),(1,)),((),())),preferred_element_type=f32)
def dot_tn(a,b): return lax.dot_general(a,b,(((0,),(0,)),((),())),preferred_element_type=f32)
def split(x):
    hi=x.astype(bf16); return hi,(x-hi.astype(f32)).astype(bf16)
def masks(C):
    i=lax.broadcasted_iota(jnp.int32,(C,C),0); j=lax.broadcasted_iota(jnp.int32,(C,C),1)
    ms=[((i//8)==(j//8)).astype(bf16)]
    s=8
    while s<C:
        ms.append((((i//(2*s))==(j//(2*s))) & ((i//s)!=(j//s))).astype(bf16)); s*=2
    eye=(i==j).astype(f32)
    return ms,eye
def inverse(A,ms,eye,mode):
    if mode=="f32":
        out=[]
        for a in A:
            out.append(jax.scipy.linalg.solve_triangular(a+eye,eye,lower=True,unit_diagonal=True))
        return out
    if mode.startswith("bf"):
        Ab=[a.astype(bf16) for a in A]
        A8=[a*ms[0] for a in Ab]
        P=[dot(a,a).astype(bf16) for a in A8]
        IA=[(eye.astype(bf16)-a) for a in A8]
        X1=[x.astype(f32)+dot(x,p) for x,p in zip(IA,P)]
        P2=[dot(p,p).astype(bf16) for p in P]
        X=[x+dot(x.astype(bf16),p) for x,p in zip(X1,P2)]
        for m in ms[1:]:
            Xb=[x.astype(bf16) for x in X]
            B=[dot(a*m,x).astype(bf16) for a,x in zip(Ab,Xb)]
            X=[x-dot(xb,b) for x,xb,b in zip(X,Xb,B)]
        nref=int(mode[2:])
        for r in range(nref):
            X0=[x.astype(bf16) for x in X]
            if r==0: As=[jnp.concatenate(split(a),axis=1) for a in A]
            if r==0 or True:
                E=[(eye-x.astype(f32))-dot(a,jnp.concatenate([x,x],axis=0)) for a,x in zip(As,X0)]
            X=[x.astype(f32)+dot(x,e.astype(bf16)) for x,e in zip(X0,E)]
        return X
def chunk(Y,k,q,v,Lr,Lc,br,bc,Lq,ms,eye,mode="bf1",opt=()):
    C=k[0].shape[0]; T=q[0].shape[0]; d=k[0].shape[1]; n=len(k)
    i=lax.broadcasted_iota(jnp.int32,(C+T,C),0); j=lax.broadcasted_iota(jnp.int32,(C+T,C),1)
    lim=jnp.where(i<C,i-1,2*(i-C)+1)
    mask=j<=lim
    H=range(n)
    G=[dot_nt(jnp.concatenate([k[h],q[h]],0),k[h]) for h in H]
    Gd=[G[h][:C]*eye for h in H]
    nr=[lax.rsqrt(jnp.sum(Gd[h],axis=0,keepdims=True)+1e-6) for h in H]
    nc=[lax.rsqrt(jnp.sum(Gd[h],axis=1,keepdims=True)+1e-6) for h in H]
    qn=[lax.rsqrt(jnp.sum(jnp.square(q[h].astype(f32)),axis=1,keepdims=True)+1e-6) for h in H]
    lev=[jnp.concatenate([Lc[h],Lq[h]],0) for h in H]
    rs=[jnp.concatenate([bc[h]*nc[h]*nc[h],qn[h]],0) for h in H]
    M=[jnp.where(mask,jnp.exp(jnp.minimum(lev[h]-Lr[h],0.0))*G[h]*rs[h],0.0) for h in H]
    A=[M[h][:C] for h in H]; wt=[M[h][C:].astype(bf16) for h in H]
    X=inverse(A,ms,eye,mode)
    bn=[br[h]*nr[h] for h in H]
    Xb=[jnp.concatenate(split(X[h]*bn[h]),1) for h in H]
    Xu=[jnp.concatenate(split(X[h]*(bn[h]*nr[h]*jnp.exp(Lr[h]))),1) for h in H]
    W=[dot(Xb[h],jnp.concatenate([v[h],v[h]],0)) for h in H]
    U=[dot(Xu[h],jnp.concatenate([k[h],k[h]],0)) for h in H]
    Us=[split(U[h]) for h in H]
    Ys=[split(Y[h]) for h in H]
    def dup(x): return jnp.concatenate([x,x],1)
    R1=[dot(dup(jnp.concatenate([Us[h][0],Us[h][1],q[h]],0)),jnp.concatenate(Ys[h],0)) for h in H]
    F=[jnp.concatenate([W[h],jnp.zeros_like(W[h])],1)-(R1[h][:C]+R1[h][C:2*C]) for h in H]
    last=[Lr[h][:,C-1:C] for h in H]
    kt=[split(jnp.transpose(k[h].astype(f32))*jnp.exp(last[h]-Lr[h])) for h in H]
    Fs=[split(F[h]) for h in H]
    ws=[split(M[h][C:]) for h in H]
    R2=[dot(dup(jnp.concatenate([kt[h][0],kt[h][1],ws[h][0],ws[h][1]],0)),jnp.concatenate(Fs[h],0)) for h in H]
    Yn=[Y[h]*jnp.exp(last[h])+(R2[h][:d]+R2[h][d:2*d]) for h in H]
    o=[(qn[h]*jnp.exp(Lq[h]))*R1[h][2*C:]+(R2[h][2*d:2*d+T]+R2[h][2*d+T:]) for h in H]
    return Yn,o


def k1_body(q_ref,k_ref,v_ref,s_ref,o_ref,qe_ref,yo_ref,y_ref,*,HB,mode):
    c=pl.program_id(1); C=k_ref.shape[0]; T=q_ref.shape[0]; d=128
    @pl.when(c==0)
    def _():
        i=lax.broadcasted_iota(jnp.int32,(d,2*d),0); j=lax.broadcasted_iota(jnp.int32,(d,2*d),1)
        y0=(j==i+d).astype(f32)
        for h in range(HB): y_ref[h]=y0
    ms,eye=masks(C)
    rows=s_ref[0]
    cols=jnp.transpose(rows)
    H=range(HB)
    sl=lambda r: [r[:,h*d:(h+1)*d] for h in H]
    P=rows.shape[0]//3
    Yn,o=chunk([y_ref[h] for h in H],sl(k_ref),sl(q_ref),sl(v_ref),
        [rows[h:h+1] for h in H],[cols[:,h:h+1] for h in H],
        [rows[P+h:P+h+1] for h in H],[cols[:,P+h:P+h+1] for h in H],
        [cols[:T,2*P+h:2*P+h+1] for h in H],ms,eye,mode)
    for h in H:
        y_ref[h]=Yn[h]
        o_ref[:,h*d:(h+1)*d]=o[h][:,:d]
        qe_ref[:,h*d:(h+1)*d]=o[h][:,d:].astype(bf16)
    @pl.when(c==pl.num_programs(1)-1)
    def _():
        for h in H: yo_ref[h]=Yn[h]
def small(betas,log_decay,HB,T=64):
    n,heads=log_decay.shape
    ch=n//T
    L=jnp.cumsum(log_decay.reshape(ch,T,heads),axis=1).transpose(0,2,1)
    L2=jnp.repeat(L,2,axis=2)
    b=betas.reshape(ch,2*T,heads).transpose(0,2,1)
    Lp=jnp.concatenate([L,jnp.zeros_like(L)],axis=2)
    P=max(HB,8)
    out=jnp.stack([L2,b,Lp],1)
    g=heads//HB
    out=out.reshape(ch,3,g,HB,2*T).transpose(2,0,1,3,4)
    if HB<8: out=jnp.concatenate([out,jnp.zeros((g,ch,3,8-HB,2*T),f32)],3)
    return out.reshape(g*ch,3*P,2*T)
def k1(queries,keys2,values2,sm,HB,mode="bf1",T=64):
    n=queries.shape[0]; heads=queries.shape[1]//128; ch=n//T; g=heads//HB; w=HB*128
    return pl.pallas_call(functools.partial(k1_body,HB=HB,mode=mode),
        grid=(g,ch),
        in_specs=[pl.BlockSpec((T,w),lambda i,c:(c,i)),pl.BlockSpec((2*T,w),lambda i,c:(c,i)),pl.BlockSpec((2*T,w),lambda i,c:(c,i)),
                  pl.BlockSpec((1,)+sm.shape[1:],lambda i,c:(i*ch+c,0,0))],
        out_specs=[pl.BlockSpec((T,w),lambda i,c:(c,i)),pl.BlockSpec((T,w),lambda i,c:(c,i)),pl.BlockSpec((HB,128,256),lambda i,c:(i,0,0))],
        out_shape=[jax.ShapeDtypeStruct((n,heads*128),f32),jax.ShapeDtypeStruct((n,heads*128),bf16),jax.ShapeDtypeStruct((heads,128,256),f32)],
        scratch_shapes=[pltpu.VMEM((HB,128,256),f32)],
        compiler_params=pltpu.CompilerParams(vmem_limit_bytes=50*2**20),
        name="local_chunks",
    )(queries,keys2,values2,sm)


def attend_body(q_ref, kp_ref, ko_ref, vp_ref, vo_ref, out_ref, *, HB, axis, R):
    n = q_ref.shape[0]
    d = 128
    bias = jnp.where(lax.axis_index(axis) > 0, 0.0, -1e30).astype(f32)
    scale = d ** -0.5 * math.log2(math.e)
    ones = jnp.ones((n, d), bf16)
    tri = lax.broadcasted_iota(jnp.int32, (R, R), 1) <= lax.broadcasted_iota(jnp.int32, (R, R), 0)
    for h in range(HB):
        s = slice(h * d, h * d + d)
        vp = jnp.concatenate([vp_ref[:, s], ones], 1)
        vo = jnp.concatenate([vo_ref[:, s], ones], 1)
        for i in range(n // R):
            q = q_ref[i * R:(i + 1) * R, s]
            sp = dot_nt(q, kp_ref[:, s]) + bias
            so = dot_nt(q, ko_ref[: (i + 1) * R, s])
            diag = jnp.where(tri, so[:, i * R:], -1e30)
            so = diag if i == 0 else jnp.concatenate([so[:, : i * R], diag], 1)
            m = jnp.maximum(jnp.max(sp, 1, keepdims=True), jnp.max(so, 1, keepdims=True))
            ep = jnp.exp2((sp - m) * scale).astype(bf16)
            eo = jnp.exp2((so - m) * scale).astype(bf16)
            r = dot(ep, vp) + dot(eo, vo[: (i + 1) * R])
            out_ref[i * R:(i + 1) * R, s] = (r[:, :d] / r[:, d:]).astype(bf16)

def attend(q, kp, ko, vp, vo, HB=1, R=256, axis="ctx"):
    n, w = q.shape
    spec = pl.BlockSpec((n, HB * 128), lambda h: (0, h))
    return pl.pallas_call(
        functools.partial(attend_body, HB=HB, axis=axis, R=R), grid=(w // (HB * 128),),
        in_specs=[spec] * 5, out_specs=spec, out_shape=jax.ShapeDtypeStruct((n, w), bf16),
        compiler_params=pltpu.CompilerParams(vmem_limit_bytes=50 * 2**20), name="attend")(q, kp, ko, vp, vo)

def finish_body(o_ref, qe_ref, z_ref, out_ref, *, HB):
    d = 128
    for h in range(HB):
        s = slice(h * d, h * d + d)
        out_ref[:, s] = (o_ref[:, s] + dot(qe_ref[:, s], z_ref[h])).astype(bf16)

def finish(o, qe, z, B=128):
    n, w = o.shape
    spec = pl.BlockSpec((B, w), lambda i: (i, 0))
    return pl.pallas_call(
        functools.partial(finish_body, HB=w // 128), grid=(n // B,),
        in_specs=[spec, spec, pl.BlockSpec(z.shape, lambda i: (0, 0, 0))], out_specs=spec,
        out_shape=jax.ShapeDtypeStruct((n, w), bf16), name="finish")(o, qe, z)

def hop_body(y_ref, z_ref, out_ref):
    d = 128
    for h in range(y_ref.shape[0]):
        y = y_ref[h]
        hi, lo = split(y[:, d:])
        z = z_ref[h]
        out_ref[h] = (y[:, :d] + dot(jnp.concatenate([hi, lo], 1), jnp.concatenate([z, z], 0))).astype(bf16)

def hop(y, z):
    return pl.pallas_call(hop_body, out_shape=jax.ShapeDtypeStruct(z.shape, bf16), name="hop")(y, z)


def from_behind(array, axis, by):
    n = lax.axis_size(axis)
    return lax.ppermute(array, axis, [(i, i + by) for i in range(n) if 0 <= i + by < n])
def per_device(queries, keys, values, betas, log_decay, attn_queries, attn_keys):
    n, w = queries.shape
    ak_prev = from_behind(attn_keys, "ctx", 1)
    HB = min(8, w // 128)
    sm = small(betas, log_decay, HB)
    o, qe, y = k1(queries, keys.reshape(2 * n, w), values.reshape(2 * n, w), sm, HB)
    z = y[:, :, :128].astype(bf16)
    z = from_behind(z, "ctx", 1)
    for _ in range(lax.axis_size("ctx") - 2):
        z = from_behind(hop(y, z), "ctx", 1)
    ret = finish(o, qe, z)
    rp = from_behind(ret, "ctx", 1)
    return ret, attend(attn_queries, ak_prev, attn_keys, rp, ret)


def solution(mesh):
    rows, cols = ("groups", "ctx"), ("head", "sub")
    flat, paired = P(rows, cols), P(rows, None, cols)
    return jax.shard_map(
        per_device,
        mesh=mesh,
        in_specs=(flat, paired, paired, paired, flat, flat, flat),
        out_specs=(flat, flat),
        check_vma=False,
    )
```

```python
import functools
import math

import jax
import jax.numpy as jnp
from jax import lax
from jax.experimental import pallas as pl
from jax.experimental.pallas import tpu as pltpu
from jax.sharding import PartitionSpec as P

f32 = jnp.float32
bf16 = jnp.bfloat16


def dot(a, b):
    return lax.dot_general(a, b, (((1,), (0,)), ((), ())), preferred_element_type=f32)


def dot_nt(a, b):
    return lax.dot_general(a, b, (((1,), (1,)), ((), ())), preferred_element_type=f32)


def cat(parts, axis):
    return jnp.concatenate(parts, axis)


def split(x):
    hi = x.astype(bf16)
    return hi, (x - hi.astype(f32)).astype(bf16)


def product(a, b):
    n = b[0].shape[1]
    row = cat(b, 1)
    r = dot(cat(a, 1), cat([row, row], 0))
    return r[:, :n] + r[:, n:]


def odd(x, s):
    return cat([x[b * s:(b + 1) * s] for b in range(1, x.shape[0] // s, 2)], 0)


def weave(even, o, s):
    out = []
    for b in range(o.shape[0] // s):
        out.append(jnp.zeros((s, o.shape[1]), o.dtype) if even is None else even[2 * b * s:(2 * b + 1) * s])
        out.append(o[b * s:(b + 1) * s])
    return cat(out, 0)


def block_masks(C):
    i = lax.broadcasted_iota(jnp.int32, (C, C), 0)
    j = lax.broadcasted_iota(jnp.int32, (C, C), 1)
    masks = {0: ((i // 4) == (j // 4)).astype(bf16)}
    s = 4
    while s < C:
        masks[s] = (((i // (2 * s)) == (j // (2 * s))) & ((i // s) != (j // s))).astype(bf16)
        s *= 2
    return masks, (i == j).astype(f32)


def inverses(A, masks, eye):
    C = eye.shape[0]
    eb = eye.astype(bf16)
    As = [split(a) for a in A]
    small = [(a[0] * masks[0], a[1] * masks[0]) for a in As]
    square = [split(product(a, a)) for a in small]
    start = [(eb - a[0], -a[1]) for a in small]
    X = [t[0].astype(f32) + t[1].astype(f32) + product(t, p) for t, p in zip(start, square)]
    Xs = [split(x) for x in X]
    s = 4
    while s < C:
        if s < 16:
            m = masks[s]
            B = [split(product((a[0] * m, a[1] * m), x)) for a, x in zip(As, Xs)]
            X = [x - product(xs, b) for x, xs, b in zip(X, Xs, B)]
            Xs = [split(x) for x in X]
        else:
            m = odd(masks[s], s)
            B = [split(product((odd(a[0], s) * m, odd(a[1], s) * m), x)) for a, x in zip(As, Xs)]
            B = [(weave(None, b[0], s), weave(None, b[1], s)) for b in B]
            Xo = [odd(x, s) - product((odd(xs[0], s), odd(xs[1], s)), b) for x, xs, b in zip(X, Xs, B)]
            X = [weave(x, o, s) for x, o in zip(X, Xo)]
            if 2 * s < C:
                So = [split(o) for o in Xo]
                Xs = [(weave(x[0], o[0], s), weave(x[1], o[1], s)) for x, o in zip(Xs, So)]
        s *= 2
    return X


def two(parts):
    x = cat(parts, 0)
    return cat([x, x], 1)


def factors(kq, k, q, v, Lr, Lc, br, bc, Lq, masks, eye):
    C, d = k[0].shape
    T = q[0].shape[0]
    H = range(len(k))
    i = lax.broadcasted_iota(jnp.int32, (C + T, C), 0)
    j = lax.broadcasted_iota(jnp.int32, (C + T, C), 1)
    visible = j <= jnp.where(i < C, i - 1, 2 * (i - C) + 1)
    nil = jnp.zeros((C, d), bf16)
    G = []
    for p, both in enumerate(kq):
        a, b = k[2 * p], k[2 * p + 1]
        r = dot_nt(both, cat([cat([a, nil], 1), cat([nil, b], 1)], 0))
        G += [r[:, :C], r[:, C:]]
    Gd = [G[h][:C] * eye for h in H]
    nr = [lax.rsqrt(jnp.sum(Gd[h], axis=0, keepdims=True) + 1e-6) for h in H]
    nc = [lax.rsqrt(jnp.sum(Gd[h], axis=1, keepdims=True) + 1e-6) for h in H]
    qn = [lax.rsqrt(jnp.sum(jnp.square(q[h].astype(f32)), axis=1, keepdims=True) + 1e-6) for h in H]
    lev = [cat([Lc[h], Lq[h]], 0) for h in H]
    rs = [cat([bc[h] * nc[h] * nc[h], qn[h]], 0) for h in H]
    M = [jnp.where(visible, jnp.exp(jnp.minimum(lev[h] - Lr[h], 0.0)) * G[h] * rs[h], 0.0) for h in H]
    X = inverses([M[h][:C] for h in H], masks, eye)
    bn = [br[h] * nr[h] for h in H]
    W = [dot(cat(split(X[h] * bn[h]), 1), cat([v[h], v[h]], 0)) for h in H]
    U = [dot(cat(split(X[h] * (bn[h] * nr[h] * jnp.exp(Lr[h]))), 1), cat([k[h], k[h]], 0)) for h in H]
    last = [Lr[h][:, C - 1:C] for h in H]
    kt = [split(jnp.transpose(k[h].astype(f32)) * jnp.exp(last[h] - Lr[h])) for h in H]
    ws = [split(M[h][C:]) for h in H]
    right = [split(cat([U[h], W[h]], 1)) for h in H]
    R = [dot(two([kt[h][0], ws[h][0], kt[h][1], ws[h][1]]), cat(right[h], 0)) for h in H]
    R = [r[:d + T] + r[d + T:] for r in R]
    left = [split(cat([R[h][:d, :d], (qn[h] * jnp.exp(Lq[h])) * q[h].astype(f32) - R[h][d:, :d]], 0)) for h in H]
    return left, [R[h][:, d:] for h in H], [jnp.exp(last[h]) for h in H]


def advance(Y, left, add, decay):
    H = range(len(Y))
    d = Y[0].shape[0]
    n = left[0][0].shape[0]
    R = [dot(two(left[h]), cat(split(Y[h]), 0)) for h in H]
    R = [r[:n] + r[n:] for r in R]
    nil = jnp.zeros_like(add[0])
    own = [cat([a, nil], 1) for a in add]
    return [Y[h] * decay[h] + own[h][:d] - R[h][:d] for h in H], [own[h][d:] + R[h][d:] for h in H]


D = 128


def params(mib):
    return pltpu.CompilerParams(vmem_limit_bytes=mib * 2**20)


def cost(us):
    return pl.CostEstimate(flops=int(us * 10**9), bytes_accessed=10**6, transcendentals=0)


def local_body(q_ref, k_ref, v_ref, b_ref, l_ref, o_ref, qe_ref, yo_ref, a_ref, y_ref, r_ref, *, HB, NC, first):
    c = pl.program_id(0)
    T = q_ref.shape[0] // NC
    C = 2 * T
    d = D
    H = range(HB)
    heads = l_ref.shape[0]

    @pl.when(c == 0)
    def _():
        i = lax.broadcasted_iota(jnp.int32, (d, 2 * d), 0)
        j = lax.broadcasted_iota(jnp.int32, (d, 2 * d), 1)
        for h in H:
            y_ref[h] = (j == i + d).astype(f32)

        def pick(x, m):
            a = x.astype(bf16)
            r = dot(cat([a, *split(x - a.astype(f32))], 0), m.astype(bf16))
            return r[:heads] + r[heads:2 * heads] + r[2 * heads:]

        def full(x):
            return x if heads == 8 else cat([x, jnp.zeros((8 - heads, C), f32)], 0)

        ld, b0, b1 = l_ref[...], b_ref[0], b_ref[1]
        t = lax.broadcasted_iota(jnp.int32, (l_ref.shape[1], C), 0)
        i = lax.broadcasted_iota(jnp.int32, (l_ref.shape[1], C), 1)
        for s in range(r_ref.shape[0]):
            u = t - s * T
            r_ref[s, 0:8] = full(pick(ld, (u >= 0) & (u <= i // 2)))
            r_ref[s, 8:16] = full(pick(b0, 2 * u == i) + pick(b1, 2 * u + 1 == i))
            r_ref[s, 16:24] = full(pick(ld, (u >= 0) & (u <= i)))

    masks, eye = block_masks(C)
    kq, k, q, v, Lr, Lc, br, bc, Lq = ([] for _ in range(9))
    for s in range(NC):
        rows = r_ref[c * NC + s]
        cols = jnp.transpose(cat([rows, jnp.zeros((C - 24, C), f32)], 0))
        ks = k_ref[s * T:(s + 1) * T].reshape(C, HB * d)
        vs = v_ref[s * T:(s + 1) * T].reshape(C, HB * d)
        qs = q_ref[s * T:(s + 1) * T]
        both = cat([ks, qs], 0)
        kq += [both[:, p * d:(p + 2) * d] for p in range(0, HB, 2)]
        for h in H:
            at = first + h
            k.append(ks[:, h * d:(h + 1) * d])
            v.append(vs[:, h * d:(h + 1) * d])
            q.append(qs[:, h * d:(h + 1) * d])
            Lr.append(rows[at:at + 1])
            br.append(rows[8 + at:9 + at])
            Lc.append(cols[:, at:at + 1])
            bc.append(cols[:, 8 + at:9 + at])
            Lq.append(cols[:T, 16 + at:17 + at])
    left, add, decay = factors(kq, k, q, v, Lr, Lc, br, bc, Lq, masks, eye)
    Y = [y_ref[h] for h in H]
    for s in range(NC):
        now = slice(s * HB, (s + 1) * HB)
        Y, o = advance(Y, left[now], add[now], decay[now])
        for h in H:
            o_ref[s * T:(s + 1) * T, h * d:(h + 1) * d] = o[h][:, :d]
            qe_ref[s * T:(s + 1) * T, h * d:(h + 1) * d] = o[h][:, d:].astype(bf16)
    for h in H:
        y_ref[h] = Y[h]

    @pl.when(c == pl.num_programs(0) - 1)
    def _():
        for h in H:
            yo_ref[h] = Y[h]
            a_ref[h] = Y[h][:, :d].astype(bf16)


def local(queries, keys, values, betas, decay, g, HB, NC, T=64):
    n, w = queries.shape
    heads = w // D
    wg = HB * D
    B = NC * T
    flat = pl.BlockSpec((B, wg), lambda c: (c, g))
    pair = pl.BlockSpec((B, 2, wg), lambda c: (c, 0, g))
    out = pl.BlockSpec((B, wg), lambda c: (c, 0))
    whole = lambda *s: pl.BlockSpec(s, lambda c: (0,) * len(s))
    return pl.pallas_call(
        functools.partial(local_body, HB=HB, NC=NC, first=g * HB),
        grid=(n // B,),
        in_specs=[flat, pair, pair, whole(2, heads, n), whole(heads, n)],
        out_specs=[out, out, whole(HB, D, 2 * D), whole(HB, D, D)],
        out_shape=[jax.ShapeDtypeStruct((n, wg), f32), jax.ShapeDtypeStruct((n, wg), bf16), jax.ShapeDtypeStruct((HB, D, 2 * D), f32), jax.ShapeDtypeStruct((HB, D, D), bf16)],
        scratch_shapes=[pltpu.VMEM((HB, D, 2 * D), f32), pltpu.VMEM((n // T, 24, 2 * T), f32)],
        cost_estimate=cost(HB * 5), name="local", compiler_params=params(52),
    )(queries, keys, values, betas, decay)


VMEM = pl.BlockSpec(memory_space=pltpu.VMEM)


def hop_body(y_ref, z_ref, out_ref):
    for h in range(y_ref.shape[0]):
        hi, lo = split(y_ref[h, :, D:])
        z = z_ref[h]
        out_ref[h] = (y_ref[h, :, :D] + dot(cat([hi, lo], 1), cat([z, z], 0))).astype(bf16)


def hop(y, z):
    return pl.pallas_call(
        hop_body, in_specs=[VMEM, VMEM], out_specs=VMEM, out_shape=jax.ShapeDtypeStruct(z.shape, bf16),
        cost_estimate=cost(1), name="hop", compiler_params=params(8))(y, z)


def finish_body(o_ref, qe_ref, z_ref, out_ref):
    for h in range(z_ref.shape[0]):
        s = slice(h * D, h * D + D)
        out_ref[:, s] = (o_ref[:, s] + dot(qe_ref[:, s], z_ref[h])).astype(bf16)


def finish(o, qe, z, B=256):
    n, w = o.shape
    spec = pl.BlockSpec((B, w), lambda i: (i, 0))
    return pl.pallas_call(
        finish_body, grid=(n // B,), in_specs=[spec, spec, VMEM], out_specs=spec,
        out_shape=jax.ShapeDtypeStruct((n, w), bf16), cost_estimate=cost(2), name="finish", compiler_params=params(8))(o, qe, z)


def attend_body(q_ref, kp_ref, ko_ref, vp_ref, o_ref, qe_ref, z_ref, *refs, axis, R, first):
    ret_ref, out_ref = refs[-2:]
    n = q_ref.shape[0]
    h = pl.program_id(0)
    bias = jnp.where(lax.axis_index(axis) > 0, 0.0, -1e30).astype(f32)
    scale = D ** -0.5 * math.log2(math.e)
    ones = jnp.ones((n, D), bf16)
    tri = lax.broadcasted_iota(jnp.int32, (R, R), 1) <= lax.broadcasted_iota(jnp.int32, (R, R), 0)
    ret = (o_ref[...] + dot(qe_ref[...], z_ref[h])).astype(bf16)
    ret_ref[...] = ret
    kp = kp_ref[:, pl.ds(pl.multiple_of(h * D, D), D)]
    vp = cat([vp_ref[:, pl.ds(pl.multiple_of(h * D, D), D)], ones], 1)
    vo = cat([ret, ones], 1)
    for i in range(n // R):
        q = q_ref[i * R:(i + 1) * R]
        sp = dot_nt(q, kp) + bias
        so = dot_nt(q, ko_ref[:(i + 1) * R])
        diag = jnp.where(tri, so[:, i * R:], -1e30)
        so = diag if i == 0 else cat([so[:, :i * R], diag], 1)
        m = jnp.maximum(jnp.max(sp, 1, keepdims=True), jnp.max(so, 1, keepdims=True))
        ep = jnp.exp2((sp - m) * scale).astype(bf16)
        eo = jnp.exp2((so - m) * scale).astype(bf16)
        r = dot(ep, vp) + dot(eo, vo[:(i + 1) * R])
        out_ref[i * R:(i + 1) * R] = (r[:, :D] / r[:, D:]).astype(bf16)


def attend(q, kp, ko, vp, o, qe, z, carry, g, HB, R=256, axis="ctx"):
    n, w = q.shape
    flat = pl.BlockSpec((n, D), lambda h: (0, g * HB + h))
    part = pl.BlockSpec((n, D), lambda h: (0, h))
    held = [pl.BlockSpec(memory_space=pl.ANY)] * len(carry)
    return pl.pallas_call(
        functools.partial(attend_body, axis=axis, R=R, first=g * HB), grid=(HB,),
        in_specs=[flat, VMEM, flat, VMEM, part, part, VMEM] + held, out_specs=[flat, flat],
        out_shape=[jax.ShapeDtypeStruct((n, w), bf16)] * 2,
        input_output_aliases={7 + i: i for i in range(len(carry))},
        cost_estimate=cost(HB * 1.3), name="attend", compiler_params=params(24))(q, kp, ko, vp, o, qe, z, *carry)


def from_behind(array, axis):
    n = lax.axis_size(axis)
    return lax.ppermute(array, axis, [(i, i + 1) for i in range(n - 1)])


GROUPS = 2


def per_device(queries, keys, values, betas, log_decay, attn_queries, attn_keys):
    n, w = queries.shape
    HB = w // D // GROUPS
    hops = lax.axis_size("ctx") - 1
    G = range(GROUPS)
    beta_rows = betas.transpose(1, 2, 0)
    decay_rows = log_decay.transpose(1, 0)
    keys_behind = []
    parts = []
    for g in G:
        if g:
            decay_rows, keys_behind[-1] = lax.optimization_barrier((decay_rows, keys_behind[-1]))
        keys_behind.append(from_behind(attn_keys[:, g * HB * D:(g + 1) * HB * D], "ctx"))
        parts.append(local(queries, keys, values, beta_rows, decay_rows, g, HB, math.gcd(16 // HB, n // 64)))
    z = [jnp.zeros_like(p[3]) for p in parts]
    behind = [None] * GROUPS
    for k in range(hops):
        for g in G:
            o, qe, y, a = parts[g]
            if k == 1 and g < GROUPS - 1:
                z[g], parts[-1], keys_behind[-1] = lax.optimization_barrier((z[g], parts[-1], keys_behind[-1]))
                o, qe, y, a = parts[g]
            sent = a if k == 0 else hop(y, z[g])
            if k == hops - 1:
                ret = finish(o, qe, z[g])
            z[g] = from_behind(sent, "ctx")
            if k == hops - 1:
                behind[g] = from_behind(ret, "ctx")
    carry = ()
    for g in G:
        o, qe, y, a = parts[g]
        carry = attend(attn_queries, keys_behind[g], attn_keys, behind[g], o, qe, z[g], carry, g, HB)
    return tuple(carry)


def solution(mesh):
    rows, cols = ("groups", "ctx"), ("head", "sub")
    flat, paired = P(rows, cols), P(rows, None, cols)
    return jax.shard_map(
        per_device,
        mesh=mesh,
        in_specs=(flat, paired, paired, paired, flat, flat, flat),
        out_specs=(flat, flat),
        check_vma=False,
    )
```

```python
import functools
import math

import jax
import jax.numpy as jnp
from jax import lax
from jax.experimental import pallas as pl
from jax.experimental.pallas import tpu as pltpu
from jax.sharding import PartitionSpec as P

f32 = jnp.float32
bf16 = jnp.bfloat16


def dot(a, b):
    return lax.dot_general(a, b, (((1,), (0,)), ((), ())), preferred_element_type=f32)


def dot_nt(a, b):
    return lax.dot_general(a, b, (((1,), (1,)), ((), ())), preferred_element_type=f32)


def cat(parts, axis):
    return jnp.concatenate(parts, axis)


def split(x):
    hi = x.astype(bf16)
    return hi, (x - hi.astype(f32)).astype(bf16)


def product(a, b):
    n = b[0].shape[1]
    row = cat(b, 1)
    r = dot(cat(a, 1), cat([row, row], 0))
    return r[:, :n] + r[:, n:]


def odd(x, s):
    return cat([x[b * s:(b + 1) * s] for b in range(1, x.shape[0] // s, 2)], 0)


def weave(even, o, s):
    out = []
    for b in range(o.shape[0] // s):
        out.append(jnp.zeros((s, o.shape[1]), o.dtype) if even is None else even[2 * b * s:(2 * b + 1) * s])
        out.append(o[b * s:(b + 1) * s])
    return cat(out, 0)


def block_masks(C):
    i = lax.broadcasted_iota(jnp.int32, (C, C), 0)
    j = lax.broadcasted_iota(jnp.int32, (C, C), 1)
    masks = {}
    s = BASE
    while s < C:
        masks[s] = (((i // (2 * s)) == (j // (2 * s))) & ((i // s) != (j // s))).astype(bf16)
        s *= 2
    return masks, (i == j).astype(f32)


BASE = 16


def base_inverses(A):
    C = A[0].shape[0]
    i = lax.broadcasted_iota(jnp.int32, (C, C), 0)
    j = lax.broadcasted_iota(jnp.int32, (C, C), 1)
    place = (j // BASE - i // BASE) & (C // BASE - 1)
    first = j & ~(BASE - 1)
    zero = jnp.zeros((C, C), f32)
    halves = lambda x: [x.reshape(C // BASE, BASE, C)[:, r:r + 8] for r in (0, 8)]
    packs = []
    for at in range(0, len(A), C // BASE):
        packed = zero
        for p, a in enumerate(A[at:at + C // BASE]):
            packed = jnp.where(place == p, pltpu.roll(a, BASE * p, 1) if p else a, packed)
        packs.append(packed)
    start = halves(((j & (BASE - 1)) == (i & (BASE - 1))).astype(f32))
    X = [list(start) for _ in packs]
    for k in range(BASE - 1):
        for x, packed in zip(X, packs):
            lo, hi = halves(jnp.take_along_axis(packed, first + k, axis=1))
            row = x[k // 8][:, k % 8:k % 8 + 1]
            if k < 7:
                x[0] = x[0] - lo * row
            x[1] = x[1] - hi * row
    out = []
    for x, at in zip(X, range(0, len(A), C // BASE)):
        whole = jnp.concatenate(x, axis=1).reshape(C, C)
        for p in range(min(len(A) - at, C // BASE)):
            out.append(jnp.where(place == 0, pltpu.roll(whole, C - BASE * p, 1) if p else whole, zero))
    return out


def inverses(A, masks, eye):
    C = eye.shape[0]
    As = [split(a) for a in A]
    X = base_inverses(A)
    Xs = [split(x) for x in X]
    s = BASE
    while s < C:
        m = odd(masks[s], s)
        B = [split(product((odd(a[0], s) * m, odd(a[1], s) * m), x)) for a, x in zip(As, Xs)]
        B = [(weave(None, b[0], s), weave(None, b[1], s)) for b in B]
        Xo = [odd(x, s) - product((odd(xs[0], s), odd(xs[1], s)), b) for x, xs, b in zip(X, Xs, B)]
        X = [weave(x, o, s) for x, o in zip(X, Xo)]
        if 2 * s < C:
            So = [split(o) for o in Xo]
            Xs = [(weave(x[0], o[0], s), weave(x[1], o[1], s)) for x, o in zip(Xs, So)]
        s *= 2
    return X


def two(parts):
    x = cat(parts, 0)
    return cat([x, x], 1)


def factors(kq, k, q, v, Lr, Lc, br, bc, Lq, masks, eye):
    C, d = k[0].shape
    T = q[0].shape[0]
    H = range(len(k))
    i = lax.broadcasted_iota(jnp.int32, (C + T, C), 0)
    j = lax.broadcasted_iota(jnp.int32, (C + T, C), 1)
    visible = j <= jnp.where(i < C, i - 1, 2 * (i - C) + 1)
    nil = jnp.zeros((C, d), bf16)
    G = []
    for p, both in enumerate(kq):
        a, b = k[2 * p], k[2 * p + 1]
        r = dot_nt(both, cat([cat([a, nil], 1), cat([nil, b], 1)], 0))
        G += [r[:, :C], r[:, C:]]
    Gd = [G[h][:C] * eye for h in H]
    nr = [lax.rsqrt(jnp.sum(Gd[h], axis=0, keepdims=True) + 1e-6) for h in H]
    nc = [lax.rsqrt(jnp.sum(Gd[h], axis=1, keepdims=True) + 1e-6) for h in H]
    qn = [lax.rsqrt(jnp.sum(jnp.square(q[h].astype(f32)), axis=1, keepdims=True) + 1e-6) for h in H]
    lev = [cat([Lc[h], Lq[h]], 0) for h in H]
    rs = [cat([bc[h] * nc[h] * nc[h], qn[h]], 0) for h in H]
    M = [jnp.where(visible, jnp.exp(jnp.minimum(lev[h] - Lr[h], 0.0)) * G[h] * rs[h], 0.0) for h in H]
    X = inverses([M[h][:C] for h in H], masks, eye)
    bn = [br[h] * nr[h] for h in H]
    W = [dot(cat(split(X[h] * bn[h]), 1), cat([v[h], v[h]], 0)) for h in H]
    U = [dot(cat(split(X[h] * (bn[h] * nr[h] * jnp.exp(Lr[h]))), 1), cat([k[h], k[h]], 0)) for h in H]
    last = [Lr[h][:, C - 1:C] for h in H]
    kt = [split(jnp.transpose(k[h].astype(f32)) * jnp.exp(last[h] - Lr[h])) for h in H]
    ws = [split(M[h][C:]) for h in H]
    right = [split(cat([U[h], W[h]], 1)) for h in H]
    R = [dot(two([kt[h][0], ws[h][0], kt[h][1], ws[h][1]]), cat(right[h], 0)) for h in H]
    R = [r[:d + T] + r[d + T:] for r in R]
    left = [split(cat([R[h][:d, :d], (qn[h] * jnp.exp(Lq[h])) * q[h].astype(f32) - R[h][d:, :d]], 0)) for h in H]
    return left, [R[h][:, d:] for h in H], [jnp.exp(last[h]) for h in H]


def advance(Y, left, add, decay):
    H = range(len(Y))
    d = Y[0].shape[0]
    n = left[0][0].shape[0]
    R = [dot(two(left[h]), cat(split(Y[h]), 0)) for h in H]
    R = [r[:n] + r[n:] for r in R]
    nil = jnp.zeros_like(add[0])
    own = [cat([a, nil], 1) for a in add]
    return [Y[h] * decay[h] + own[h][:d] - R[h][:d] for h in H], [own[h][d:] + R[h][d:] for h in H]


D = 128
LOCAL = 1


def params(mib):
    return pltpu.CompilerParams(vmem_limit_bytes=mib * 2**20)


def cost(us):
    return pl.CostEstimate(flops=int(us * 10**9), bytes_accessed=10**6, transcendentals=0)


def local_body(q_ref, k_ref, v_ref, b_ref, l_ref, o_ref, qe_ref, yo_ref, am_ref, a_ref, y_ref, r_ref, *, HB, NC, first):
    c = pl.program_id(0)
    T = q_ref.shape[0] // NC
    C = 2 * T
    d = D
    H = range(HB)
    heads = l_ref.shape[0]

    @pl.when(c == 0)
    def _():
        i = lax.broadcasted_iota(jnp.int32, (d, 2 * d), 0)
        j = lax.broadcasted_iota(jnp.int32, (d, 2 * d), 1)
        for h in H:
            y_ref[h] = (j == i + d).astype(f32)

        def pick(x, m):
            a = x.astype(bf16)
            r = dot(cat([a, *split(x - a.astype(f32))], 0), m.astype(bf16))
            return r[:heads] + r[heads:2 * heads] + r[2 * heads:]

        def full(x):
            return x if heads == 8 else cat([x, jnp.zeros((8 - heads, C), f32)], 0)

        ld, b0, b1 = l_ref[...], b_ref[0], b_ref[1]
        t = lax.broadcasted_iota(jnp.int32, (l_ref.shape[1], C), 0)
        i = lax.broadcasted_iota(jnp.int32, (l_ref.shape[1], C), 1)
        for s in range(r_ref.shape[0]):
            u = t - s * T
            r_ref[s, 0:8] = full(pick(ld, (u >= 0) & (u <= i // 2)))
            r_ref[s, 8:16] = full(pick(b0, 2 * u == i) + pick(b1, 2 * u + 1 == i))
            r_ref[s, 16:24] = full(pick(ld, (u >= 0) & (u <= i)))

    masks, eye = block_masks(C)
    kq, k, q, v, Lr, Lc, br, bc, Lq = ([] for _ in range(9))
    for s in range(NC):
        rows = r_ref[c * NC + s]
        cols = jnp.transpose(cat([rows, jnp.zeros((C - 24, C), f32)], 0))
        ks = k_ref[s * T:(s + 1) * T].reshape(C, HB * d)
        vs = v_ref[s * T:(s + 1) * T].reshape(C, HB * d)
        qs = q_ref[s * T:(s + 1) * T]
        both = cat([ks, qs], 0)
        kq += [both[:, p * d:(p + 2) * d] for p in range(0, HB, 2)]
        for h in H:
            at = first + h
            k.append(ks[:, h * d:(h + 1) * d])
            v.append(vs[:, h * d:(h + 1) * d])
            q.append(qs[:, h * d:(h + 1) * d])
            Lr.append(rows[at:at + 1])
            br.append(rows[8 + at:9 + at])
            Lc.append(cols[:, at:at + 1])
            bc.append(cols[:, 8 + at:9 + at])
            Lq.append(cols[:T, 16 + at:17 + at])
    left, add, decay = factors(kq, k, q, v, Lr, Lc, br, bc, Lq, masks, eye)
    Y = [y_ref[h] for h in H]
    for s in range(NC):
        now = slice(s * HB, (s + 1) * HB)
        Y, o = advance(Y, left[now], add[now], decay[now])
        for h in H:
            o_ref[s * T:(s + 1) * T, h * d:(h + 1) * d] = o[h][:, :d]
            qe_ref[s * T:(s + 1) * T, h * d:(h + 1) * d] = o[h][:, d:].astype(bf16)
    for h in H:
        y_ref[h] = Y[h]

    @pl.when(c == pl.num_programs(0) - 1)
    def _():
        for h in H:
            yo_ref[h] = Y[h]
            am_ref[h] = Y[h].astype(bf16)
            a_ref[h] = Y[h][:, :d].astype(bf16)


def local(queries, keys, values, betas, decay, g, HB, NC, T=64):
    n, w = queries.shape
    heads = w // D
    wg = HB * D
    B = NC * T
    flat = pl.BlockSpec((B, wg), lambda c: (c, g))
    pair = pl.BlockSpec((B, 2, wg), lambda c: (c, 0, g))
    out = pl.BlockSpec((B, wg), lambda c: (c, 0))
    whole = lambda *s: pl.BlockSpec(s, lambda c: (0,) * len(s))
    return pl.pallas_call(
        functools.partial(local_body, HB=HB, NC=NC, first=g * HB),
        grid=(n // B,),
        in_specs=[flat, pair, pair, whole(2, heads, n), whole(heads, n)],
        out_specs=[out, out, whole(HB, D, 2 * D), whole(HB, D, 2 * D), whole(HB, D, D)],
        out_shape=[jax.ShapeDtypeStruct((n, wg), f32), jax.ShapeDtypeStruct((n, wg), bf16), jax.ShapeDtypeStruct((HB, D, 2 * D), f32), jax.ShapeDtypeStruct((HB, D, 2 * D), bf16), jax.ShapeDtypeStruct((HB, D, D), bf16)],
        scratch_shapes=[pltpu.VMEM((HB, D, 2 * D), f32), pltpu.VMEM((n // T, 24, 2 * T), f32)],
        cost_estimate=cost(HB * LOCAL), name="local", compiler_params=params(52),
    )(queries, keys, values, betas, decay)


VMEM = pl.BlockSpec(memory_space=pltpu.VMEM)


def meet_body(am_ref, a_ref, z_ref):
    for h in range(z_ref.shape[0]):
        z_ref[h] = (am_ref[h, :, :D].astype(f32) + dot(am_ref[h, :, D:], a_ref[h])).astype(bf16)


def meet(am, a):
    return pl.pallas_call(
        meet_body, in_specs=[VMEM, VMEM], out_specs=VMEM, out_shape=jax.ShapeDtypeStruct(a.shape, bf16),
        cost_estimate=cost(0.3), name="meet", compiler_params=params(8))(am, a)


def hop_body(y_ref, z_ref, out_ref):
    for h in range(y_ref.shape[0]):
        hi, lo = split(y_ref[h, :, D:])
        z = z_ref[h]
        out_ref[h] = (y_ref[h, :, :D] + dot(cat([hi, lo], 1), cat([z, z], 0))).astype(bf16)


def hop(y, z):
    return pl.pallas_call(
        hop_body, in_specs=[VMEM, VMEM], out_specs=VMEM, out_shape=jax.ShapeDtypeStruct(z.shape, bf16),
        cost_estimate=cost(0.3), name="hop", compiler_params=params(8))(y, z)


def leave_body(o_ref, qe_ref, y_ref, z_ref, out_ref):
    n = o_ref.shape[0]
    for h in range(z_ref.shape[0]):
        s = slice(h * D, h * D + D)
        z = z_ref[h]
        hi, lo = split(y_ref[h, :, D:])
        out_ref[:n, s] = (o_ref[:, s] + dot(qe_ref[:, s], z)).astype(bf16)
        out_ref[n:, s] = (y_ref[h, :, :D] + dot(cat([hi, lo], 1), cat([z, z], 0))).astype(bf16)


def leave(o, qe, y, z):
    n, w = o.shape
    return pl.pallas_call(
        leave_body, in_specs=[VMEM] * 4, out_specs=VMEM, out_shape=jax.ShapeDtypeStruct((n + D, w), bf16),
        cost_estimate=cost(0.5), name="leave", compiler_params=params(8))(o, qe, y, z)


def weigh_body(q_ref, kp_ref, ko_ref, p_ref, *, axis, R, first):
    n = q_ref.shape[0]
    h = pl.program_id(0)
    bias = jnp.where(lax.axis_index(axis) > 0, 0.0, -1e30).astype(f32)
    scale = D ** -0.5 * math.log2(math.e)
    tri = lax.broadcasted_iota(jnp.int32, (R, R), 1) <= lax.broadcasted_iota(jnp.int32, (R, R), 0)
    kp = kp_ref[:, pl.ds(pl.multiple_of((first + h) * D, D), D)]
    for i in range(n // R):
        q = q_ref[i * R:(i + 1) * R]
        sp = dot_nt(q, kp) + bias
        so = dot_nt(q, ko_ref[:(i + 1) * R])
        diag = jnp.where(tri, so[:, i * R:], -1e30)
        so = diag if i == 0 else cat([so[:, :i * R], diag], 1)
        m = jnp.maximum(jnp.max(sp, 1, keepdims=True), jnp.max(so, 1, keepdims=True))
        ep = jnp.exp2((sp - m) * scale)
        eo = jnp.exp2((so - m) * scale)
        inv = 1.0 / (jnp.sum(ep, 1, keepdims=True) + jnp.sum(eo, 1, keepdims=True))
        p_ref[0, i * R:(i + 1) * R, :n] = (ep * inv).astype(bf16)
        p_ref[0, i * R:(i + 1) * R, n:n + (i + 1) * R] = (eo * inv).astype(bf16)
        if (i + 1) * R < n:
            p_ref[0, i * R:(i + 1) * R, n + (i + 1) * R:] = jnp.zeros((R, n - (i + 1) * R), bf16)


def weigh(q, kp, ko, g, HB, R=256, axis="ctx"):
    n, w = q.shape
    flat = pl.BlockSpec((n, D), lambda h: (0, g * HB + h))
    return pl.pallas_call(
        functools.partial(weigh_body, axis=axis, R=R, first=g * HB), grid=(HB,),
        in_specs=[flat, VMEM, flat], out_specs=pl.BlockSpec((1, n, 2 * n), lambda h: (h, 0, 0)),
        out_shape=jax.ShapeDtypeStruct((HB, n, 2 * n), bf16),
        cost_estimate=cost(HB * 1.3), name="weigh", compiler_params=params(24))(q, kp, ko)


def gather_body(o_ref, qe_ref, p_ref, vz_ref, *refs):
    ret_ref, out_ref = refs[-2:]
    n = o_ref.shape[0]
    vz = vz_ref[:, pl.ds(pl.multiple_of(pl.program_id(0) * D, D), D)]
    ret = (o_ref[...] + dot(qe_ref[...], vz[n:])).astype(bf16)
    ret_ref[...] = ret
    out_ref[...] = dot(p_ref[0], cat([vz[:n], ret], 0)).astype(bf16)


def gather(o, qe, p, vz, carry, g, HB, w):
    n = o.shape[0]
    part = pl.BlockSpec((n, D), lambda h: (0, h))
    flat = pl.BlockSpec((n, D), lambda h: (0, g * HB + h))
    held = [pl.BlockSpec(memory_space=pl.ANY)] * len(carry)
    return pl.pallas_call(
        gather_body, grid=(HB,), in_specs=[part, part, pl.BlockSpec((1, n, 2 * n), lambda h: (h, 0, 0)), VMEM] + held,
        out_specs=[flat, flat], out_shape=[jax.ShapeDtypeStruct((n, w), bf16)] * 2,
        input_output_aliases={4 + i: i for i in range(len(carry))},
        cost_estimate=cost(HB * 0.5), name="gather", compiler_params=params(24))(o, qe, p, vz, *carry)


def send(array, pairs):
    return lax.ppermute(array, "ctx", pairs) if pairs else jnp.zeros_like(array)


GROUPS = 2


def per_device(queries, keys, values, betas, log_decay, attn_queries, attn_keys):
    n, w = queries.shape
    HB = w // D // GROUPS
    blocks = lax.axis_size("ctx")
    every = [(i, i + 1) for i in range(blocks - 1)]
    G = range(GROUPS)
    beta_rows = betas.transpose(1, 2, 0)
    decay_rows = log_decay.transpose(1, 0)
    keys_behind = send(attn_keys, every)
    parts, near, far, crossing = [], [], [], []
    for g in G:
        parts.append(local(queries, keys, values, beta_rows, decay_rows, g, HB, math.gcd(16 // HB, n // 64)))
        am, a = parts[g][3:]
        near.append(send(am, every[:2]))
        far.append(send(a, [(0, 2)] if blocks > 2 else []))
    for g in G:
        if g < GROUPS - 1:
            near[g], far[g], parts[-1], keys_behind = lax.optimization_barrier((near[g], far[g], parts[-1], keys_behind))
        else:
            weights = [weigh(attn_queries, keys_behind, attn_keys, h, HB) for h in G]
            near[g], far[g], weights = lax.optimization_barrier((near[g], far[g], weights))
        z = meet(near[g], far[g])
        o, qe, y = parts[g][:3]
        for k in range(3, blocks - 1):
            z = z + send(hop(y, z), [(k - 1, k)])
        crossing.append(send(leave(o, qe, y, z), every))
    done = ()
    for g in G:
        done = gather(*parts[g][:2], weights[g], crossing[g], done, g, HB, w)
    return tuple(done)


def solution(mesh):
    rows, cols = ("groups", "ctx"), ("head", "sub")
    flat, paired = P(rows, cols), P(rows, None, cols)
    return jax.shard_map(
        per_device,
        mesh=mesh,
        in_specs=(flat, paired, paired, paired, flat, flat, flat),
        out_specs=(flat, flat),
        check_vma=False,
    )
```

```python
import functools
import math

import jax
import jax.numpy as jnp
from jax import lax
from jax.experimental import pallas as pl
from jax.experimental.pallas import tpu as pltpu
from jax.sharding import PartitionSpec as P

f32 = jnp.float32
bf16 = jnp.bfloat16


def dot(a, b):
    return lax.dot_general(a, b, (((1,), (0,)), ((), ())), preferred_element_type=f32)


def dot_nt(a, b):
    return lax.dot_general(a, b, (((1,), (1,)), ((), ())), preferred_element_type=f32)


def cat(parts, axis):
    return jnp.concatenate(parts, axis)


def split(x):
    hi = x.astype(bf16)
    return hi, (x - hi.astype(f32)).astype(bf16)


def product(a, b):
    n = b[0].shape[1]
    row = cat(b, 1)
    r = dot(cat(a, 1), cat([row, row], 0))
    return r[:, :n] + r[:, n:]


def odd(x, s):
    return cat([x[b * s:(b + 1) * s] for b in range(1, x.shape[0] // s, 2)], 0)


def weave(even, o, s):
    out = []
    for b in range(o.shape[0] // s):
        out.append(jnp.zeros((s, o.shape[1]), o.dtype) if even is None else even[2 * b * s:(2 * b + 1) * s])
        out.append(o[b * s:(b + 1) * s])
    return cat(out, 0)


def block_masks(C):
    i = lax.broadcasted_iota(jnp.int32, (C, C), 0)
    j = lax.broadcasted_iota(jnp.int32, (C, C), 1)
    masks = {}
    s = BASE
    while s < C:
        masks[s] = (((i // (2 * s)) == (j // (2 * s))) & ((i // s) != (j // s))).astype(bf16)
        s *= 2
    return masks, (i == j).astype(f32)


BASE = 16


def base_inverses(A):
    C = A[0].shape[0]
    i = lax.broadcasted_iota(jnp.int32, (C, C), 0)
    j = lax.broadcasted_iota(jnp.int32, (C, C), 1)
    place = (j // BASE - i // BASE) & (C // BASE - 1)
    first = j & ~(BASE - 1)
    zero = jnp.zeros((C, C), f32)
    halves = lambda x: [x.reshape(C // BASE, BASE, C)[:, r:r + 8] for r in (0, 8)]
    packs = []
    for at in range(0, len(A), C // BASE):
        packed = zero
        for p, a in enumerate(A[at:at + C // BASE]):
            packed = jnp.where(place == p, pltpu.roll(a, BASE * p, 1) if p else a, packed)
        packs.append(packed)
    start = halves(((j & (BASE - 1)) == (i & (BASE - 1))).astype(f32))
    X = [list(start) for _ in packs]
    for k in range(BASE - 1):
        for x, packed in zip(X, packs):
            lo, hi = halves(jnp.take_along_axis(packed, first + k, axis=1))
            row = x[k // 8][:, k % 8:k % 8 + 1]
            if k < 7:
                x[0] = x[0] - lo * row
            x[1] = x[1] - hi * row
    out = []
    for x, at in zip(X, range(0, len(A), C // BASE)):
        whole = jnp.concatenate(x, axis=1).reshape(C, C)
        for p in range(min(len(A) - at, C // BASE)):
            out.append(jnp.where(place == 0, pltpu.roll(whole, C - BASE * p, 1) if p else whole, zero))
    return out


def inverses(A, masks, eye):
    C = eye.shape[0]
    As = [split(a) for a in A]
    X = base_inverses(A)
    Xs = [split(x) for x in X]
    s = BASE
    while s < C:
        m = odd(masks[s], s)
        B = [split(product((odd(a[0], s) * m, odd(a[1], s) * m), x)) for a, x in zip(As, Xs)]
        B = [(weave(None, b[0], s), weave(None, b[1], s)) for b in B]
        Xo = [odd(x, s) - product((odd(xs[0], s), odd(xs[1], s)), b) for x, xs, b in zip(X, Xs, B)]
        X = [weave(x, o, s) for x, o in zip(X, Xo)]
        if 2 * s < C:
            So = [split(o) for o in Xo]
            Xs = [(weave(x[0], o[0], s), weave(x[1], o[1], s)) for x, o in zip(Xs, So)]
        s *= 2
    return X


def two(parts):
    x = cat(parts, 0)
    return cat([x, x], 1)


def factors(kq, k, q, v, Lr, Lc, br, bc, Lq, masks, eye):
    C, d = k[0].shape
    T = q[0].shape[0]
    H = range(len(k))
    i = lax.broadcasted_iota(jnp.int32, (C + T, C), 0)
    j = lax.broadcasted_iota(jnp.int32, (C + T, C), 1)
    visible = j <= jnp.where(i < C, i - 1, 2 * (i - C) + 1)
    nil = jnp.zeros((C, d), bf16)
    G = []
    for p, both in enumerate(kq):
        a, b = k[2 * p], k[2 * p + 1]
        r = dot_nt(both, cat([cat([a, nil], 1), cat([nil, b], 1)], 0))
        G += [r[:, :C], r[:, C:]]
    Gd = [G[h][:C] * eye for h in H]
    nr = [lax.rsqrt(jnp.sum(Gd[h], axis=0, keepdims=True) + 1e-6) for h in H]
    nc = [lax.rsqrt(jnp.sum(Gd[h], axis=1, keepdims=True) + 1e-6) for h in H]
    qn = [lax.rsqrt(jnp.sum(jnp.square(q[h].astype(f32)), axis=1, keepdims=True) + 1e-6) for h in H]
    lev = [cat([Lc[h], Lq[h]], 0) for h in H]
    rs = [cat([bc[h] * nc[h] * nc[h], qn[h]], 0) for h in H]
    M = [jnp.where(visible, jnp.exp(jnp.minimum(lev[h] - Lr[h], 0.0)) * G[h] * rs[h], 0.0) for h in H]
    X = inverses([M[h][:C] for h in H], masks, eye)
    bn = [br[h] * nr[h] for h in H]
    W = [dot(cat(split(X[h] * bn[h]), 1), cat([v[h], v[h]], 0)) for h in H]
    U = [dot(cat(split(X[h] * (bn[h] * nr[h] * jnp.exp(Lr[h]))), 1), cat([k[h], k[h]], 0)) for h in H]
    last = [Lr[h][:, C - 1:C] for h in H]
    kt = [split(jnp.transpose(k[h].astype(f32)) * jnp.exp(last[h] - Lr[h])) for h in H]
    ws = [split(M[h][C:]) for h in H]
    right = [split(cat([U[h], W[h]], 1)) for h in H]
    R = [dot(two([kt[h][0], ws[h][0], kt[h][1], ws[h][1]]), cat(right[h], 0)) for h in H]
    R = [r[:d + T] + r[d + T:] for r in R]
    left = [split(cat([R[h][:d, :d], (qn[h] * jnp.exp(Lq[h])) * q[h].astype(f32) - R[h][d:, :d]], 0)) for h in H]
    return left, [R[h][:, d:] for h in H], [jnp.exp(last[h]) for h in H]


def advance(Y, left, add, decay):
    H = range(len(Y))
    d = Y[0].shape[0]
    n = left[0][0].shape[0]
    R = [dot(two(left[h]), cat(split(Y[h]), 0)) for h in H]
    R = [r[:n] + r[n:] for r in R]
    nil = jnp.zeros_like(add[0])
    own = [cat([a, nil], 1) for a in add]
    return [Y[h] * decay[h] + own[h][:d] - R[h][:d] for h in H], [own[h][d:] + R[h][d:] for h in H]


D = 128
LOCAL = 1


def params(mib):
    return pltpu.CompilerParams(vmem_limit_bytes=mib * 2**20)


def cost(us):
    return pl.CostEstimate(flops=int(us * 10**9), bytes_accessed=10**6, transcendentals=0)


def levels_body(b_ref, l_ref, r_ref, *, T):
    C = 2 * T
    heads = l_ref.shape[0]

    def pick(x, m):
        a = x.astype(bf16)
        r = dot(cat([a, *split(x - a.astype(f32))], 0), m.astype(bf16))
        return r[:heads] + r[heads:2 * heads] + r[2 * heads:]

    def full(x):
        return x if heads == 8 else cat([x, jnp.zeros((8 - heads, C), f32)], 0)

    ld, b0, b1 = l_ref[...], b_ref[0], b_ref[1]
    t = lax.broadcasted_iota(jnp.int32, (l_ref.shape[1], C), 0)
    i = lax.broadcasted_iota(jnp.int32, (l_ref.shape[1], C), 1)
    for s in range(r_ref.shape[0]):
        u = t - s * T
        r_ref[s, 0:8] = full(pick(ld, (u >= 0) & (u <= i // 2)))
        r_ref[s, 8:16] = full(pick(b0, 2 * u == i) + pick(b1, 2 * u + 1 == i))
        r_ref[s, 16:24] = full(pick(ld, (u >= 0) & (u <= i)))


def local_body(*refs, HB, NC, first, start, fresh, last):
    refs = list(refs)
    q_ref, k_ref, v_ref = refs[:3]
    y_ref = refs.pop()
    c = pl.program_id(0)
    T = q_ref.shape[0] // NC
    C = 2 * T
    d = D
    H = range(HB)
    if fresh:
        o_ref, qe_ref, r_ref, *out = refs[5:]
    else:
        r_ref, *more = refs[3:]
        if start:
            o_ref, qe_ref, *out = more[3:]
        else:
            o_ref, qe_ref, *out = more

    @pl.when(c == 0)
    def _():
        if fresh:
            levels_body(refs[3], refs[4], r_ref, T=T)
        if start:
            y_ref[...] = more[0][...]
        else:
            i = lax.broadcasted_iota(jnp.int32, (d, 2 * d), 0)
            j = lax.broadcasted_iota(jnp.int32, (d, 2 * d), 1)
            for h in H:
                y_ref[h] = (j == i + d).astype(f32)

    masks, eye = block_masks(C)
    kq, k, q, v, Lr, Lc, br, bc, Lq = ([] for _ in range(9))
    for s in range(NC):
        rows = r_ref[start + c * NC + s]
        cols = jnp.transpose(cat([rows, jnp.zeros((C - 24, C), f32)], 0))
        ks = k_ref[s * T:(s + 1) * T].reshape(C, HB * d)
        vs = v_ref[s * T:(s + 1) * T].reshape(C, HB * d)
        qs = q_ref[s * T:(s + 1) * T]
        both = cat([ks, qs], 0)
        kq += [both[:, p * d:(p + 2) * d] for p in range(0, HB, 2)]
        for h in H:
            at = first + h
            k.append(ks[:, h * d:(h + 1) * d])
            v.append(vs[:, h * d:(h + 1) * d])
            q.append(qs[:, h * d:(h + 1) * d])
            Lr.append(rows[at:at + 1])
            br.append(rows[8 + at:9 + at])
            Lc.append(cols[:, at:at + 1])
            bc.append(cols[:, 8 + at:9 + at])
            Lq.append(cols[:T, 16 + at:17 + at])
    left, add, decay = factors(kq, k, q, v, Lr, Lc, br, bc, Lq, masks, eye)
    Y = [y_ref[h] for h in H]
    for s in range(NC):
        now = slice(s * HB, (s + 1) * HB)
        Y, o = advance(Y, left[now], add[now], decay[now])
        for h in H:
            o_ref[s * T:(s + 1) * T, h * d:(h + 1) * d] = o[h][:, :d]
            qe_ref[s * T:(s + 1) * T, h * d:(h + 1) * d] = o[h][:, d:].astype(bf16)
    for h in H:
        y_ref[h] = Y[h]

    @pl.when(c == pl.num_programs(0) - 1)
    def _():
        for h in H:
            out[0][h] = Y[h]
            if last:
                out[1][h] = Y[h].astype(bf16)
                out[2][h] = Y[h][:, :d].astype(bf16)


def local(queries, keys, values, small, g, HB, start, stop, held=(), T=64):
    n, w = queries.shape
    wg = HB * D
    NC = math.gcd(16 // HB, stop - start)
    B = NC * T
    at = start // NC
    fresh, last = len(small) == 2, stop == n // T
    flat = pl.BlockSpec((B, wg), lambda c: (at + c, g))
    pair = pl.BlockSpec((B, 2, wg), lambda c: (at + c, 0, g))
    out = pl.BlockSpec((B, wg), lambda c: (at + c, 0))
    whole = lambda *s: pl.BlockSpec(s, lambda c: (0,) * len(s))
    rows = (n // T, 24, 2 * T)
    any_ = pl.BlockSpec(memory_space=pl.ANY)
    outs = [(out, (n, wg), f32), (out, (n, wg), bf16)]
    if fresh:
        outs.append((whole(*rows), rows, f32))
    outs.append((whole(HB, D, 2 * D), (HB, D, 2 * D), f32))
    if last:
        outs += [(whole(HB, D, 2 * D), (HB, D, 2 * D), bf16), (whole(HB, D, D), (HB, D, D), bf16)]
    return pl.pallas_call(
        functools.partial(local_body, HB=HB, NC=NC, first=g * HB, start=start, fresh=fresh, last=last),
        grid=((stop - start) // NC,),
        in_specs=[flat, pair, pair, *(whole(*x.shape) for x in small), *([whole(HB, D, 2 * D), any_, any_] if held else [])],
        out_specs=[x[0] for x in outs],
        out_shape=[jax.ShapeDtypeStruct(x[1], x[2]) for x in outs],
        input_output_aliases={3 + len(small) + 1: 0, 3 + len(small) + 2: 1} if held else {},
        scratch_shapes=[pltpu.VMEM((HB, D, 2 * D), f32)],
        cost_estimate=cost(HB * LOCAL), name="local", compiler_params=params(52),
    )(queries, keys, values, *small, *held)


VMEM = pl.BlockSpec(memory_space=pltpu.VMEM)


def meet_body(am_ref, a_ref, z_ref):
    for h in range(z_ref.shape[0]):
        z_ref[h] = (am_ref[h, :, :D].astype(f32) + dot(am_ref[h, :, D:], a_ref[h])).astype(bf16)


def meet(am, a):
    return pl.pallas_call(
        meet_body, in_specs=[VMEM, VMEM], out_specs=VMEM, out_shape=jax.ShapeDtypeStruct(a.shape, bf16),
        cost_estimate=cost(0.3), name="meet", compiler_params=params(8))(am, a)


def hop_body(y_ref, z_ref, out_ref):
    for h in range(y_ref.shape[0]):
        hi, lo = split(y_ref[h, :, D:])
        z = z_ref[h]
        out_ref[h] = (y_ref[h, :, :D] + dot(cat([hi, lo], 1), cat([z, z], 0))).astype(bf16)


def hop(y, z):
    return pl.pallas_call(
        hop_body, in_specs=[VMEM, VMEM], out_specs=VMEM, out_shape=jax.ShapeDtypeStruct(z.shape, bf16),
        cost_estimate=cost(0.3), name="hop", compiler_params=params(8))(y, z)


def leave_body(o_ref, qe_ref, y_ref, z_ref, out_ref):
    n = o_ref.shape[0]
    for h in range(z_ref.shape[0]):
        s = slice(h * D, h * D + D)
        z = z_ref[h]
        hi, lo = split(y_ref[h, :, D:])
        out_ref[:n, s] = (o_ref[:, s] + dot(qe_ref[:, s], z)).astype(bf16)
        out_ref[n:, s] = (y_ref[h, :, :D] + dot(cat([hi, lo], 1), cat([z, z], 0))).astype(bf16)


def leave(o, qe, y, z):
    n, w = o.shape
    return pl.pallas_call(
        leave_body, in_specs=[VMEM] * 4, out_specs=VMEM, out_shape=jax.ShapeDtypeStruct((n + D, w), bf16),
        cost_estimate=cost(0.5), name="leave", compiler_params=params(8))(o, qe, y, z)


def weigh_body(q_ref, kp_ref, ko_ref, p_ref, *, axis, R, first):
    n = q_ref.shape[0]
    h = pl.program_id(0)
    bias = jnp.where(lax.axis_index(axis) > 0, 0.0, -1e30).astype(f32)
    scale = D ** -0.5 * math.log2(math.e)
    tri = lax.broadcasted_iota(jnp.int32, (R, R), 1) <= lax.broadcasted_iota(jnp.int32, (R, R), 0)
    kp = kp_ref[:, pl.ds(pl.multiple_of((first + h) * D, D), D)]
    for i in range(n // R):
        q = q_ref[i * R:(i + 1) * R]
        sp = dot_nt(q, kp) + bias
        so = dot_nt(q, ko_ref[:(i + 1) * R])
        diag = jnp.where(tri, so[:, i * R:], -1e30)
        so = diag if i == 0 else cat([so[:, :i * R], diag], 1)
        m = jnp.maximum(jnp.max(sp, 1, keepdims=True), jnp.max(so, 1, keepdims=True))
        ep = jnp.exp2((sp - m) * scale)
        eo = jnp.exp2((so - m) * scale)
        inv = 1.0 / (jnp.sum(ep, 1, keepdims=True) + jnp.sum(eo, 1, keepdims=True))
        p_ref[0, i * R:(i + 1) * R, :n] = (ep * inv).astype(bf16)
        p_ref[0, i * R:(i + 1) * R, n:n + (i + 1) * R] = (eo * inv).astype(bf16)
        if (i + 1) * R < n:
            p_ref[0, i * R:(i + 1) * R, n + (i + 1) * R:] = jnp.zeros((R, n - (i + 1) * R), bf16)


def weigh(q, kp, ko, g, HB, R=256, axis="ctx"):
    n, w = q.shape
    flat = pl.BlockSpec((n, D), lambda h: (0, g * HB + h))
    return pl.pallas_call(
        functools.partial(weigh_body, axis=axis, R=R, first=g * HB), grid=(HB,),
        in_specs=[flat, VMEM, flat], out_specs=pl.BlockSpec((1, n, 2 * n), lambda h: (h, 0, 0)),
        out_shape=jax.ShapeDtypeStruct((HB, n, 2 * n), bf16),
        cost_estimate=cost(HB * 1), name="weigh", compiler_params=params(24))(q, kp, ko)


def gather_body(o_ref, qe_ref, p_ref, vz_ref, *refs):
    ret_ref, out_ref = refs[-2:]
    n = o_ref.shape[0]
    vz = vz_ref[:, pl.ds(pl.multiple_of(pl.program_id(0) * D, D), D)]
    ret = (o_ref[...] + dot(qe_ref[...], vz[n:])).astype(bf16)
    ret_ref[...] = ret
    out_ref[...] = dot(p_ref[0], cat([vz[:n], ret], 0)).astype(bf16)


def gather(o, qe, p, vz, carry, g, HB, w):
    n = o.shape[0]
    part = pl.BlockSpec((n, D), lambda h: (0, h))
    flat = pl.BlockSpec((n, D), lambda h: (0, g * HB + h))
    held = [pl.BlockSpec(memory_space=pl.ANY)] * len(carry)
    return pl.pallas_call(
        gather_body, grid=(HB,), in_specs=[part, part, pl.BlockSpec((1, n, 2 * n), lambda h: (h, 0, 0)), VMEM] + held,
        out_specs=[flat, flat], out_shape=[jax.ShapeDtypeStruct((n, w), bf16)] * 2,
        input_output_aliases={4 + i: i for i in range(len(carry))},
        cost_estimate=cost(HB * 0.5), name="gather", compiler_params=params(24))(o, qe, p, vz, *carry)


def send(array, pairs):
    return lax.ppermute(array, "ctx", pairs) if pairs else jnp.zeros_like(array)


def per_device(queries, keys, values, betas, log_decay, attn_queries, attn_keys):
    n, w = queries.shape
    HB = w // D // 2
    chunks = n // 64
    blocks = lax.axis_size("ctx")
    every = [(i, i + 1) for i in range(blocks - 1)]
    keys_behind = send(attn_keys, every)

    def pass_on(o, qe, y, near, far):
        z = meet(near, far)
        for k in range(3, blocks - 1):
            z = z + send(hop(y, z), [(k - 1, k)])
        return leave(o, qe, y, z)

    def round_one(am, a):
        return send(am, every[:2]), send(a, [(0, 2)] if blocks > 2 else [])

    small = (betas.transpose(1, 2, 0), log_decay.transpose(1, 0))
    o0, qe0, rows, y0, am, a = local(queries, keys, values, small, 0, HB, 0, chunks)
    near, far = round_one(am, a)
    o1, qe1, y1 = local(queries, keys, values, (rows,), 1, HB, 0, chunks // 2)
    near, far, y1 = lax.optimization_barrier((near, far, y1))
    leaving = pass_on(o0, qe0, y0, near, far)
    leaving, y1 = lax.optimization_barrier((leaving, y1))
    crossing0 = send(leaving, every)
    o1, qe1, y1, am, a = local(queries, keys, values, (rows,), 1, HB, chunks // 2, chunks, (y1, o1, qe1))
    near, far = round_one(am, a)
    keys_behind, y1 = lax.optimization_barrier((keys_behind, y1))
    weights = [weigh(attn_queries, keys_behind, attn_keys, 0, HB)]
    keys_behind, crossing0, weights = lax.optimization_barrier((keys_behind, crossing0, weights))
    weights.append(weigh(attn_queries, keys_behind, attn_keys, 1, HB))
    near, far, weights = lax.optimization_barrier((near, far, weights))
    crossing1 = send(pass_on(o1, qe1, y1, near, far), every)
    done = gather(o0, qe0, weights[0], crossing0, (), 0, HB, w)
    return tuple(gather(o1, qe1, weights[1], crossing1, tuple(done), 1, HB, w))


def solution(mesh):
    rows, cols = ("groups", "ctx"), ("head", "sub")
    flat, paired = P(rows, cols), P(rows, None, cols)
    return jax.shard_map(
        per_device,
        mesh=mesh,
        in_specs=(flat, paired, paired, paired, flat, flat, flat),
        out_specs=(flat, flat),
        check_vma=False,
    )
```

```python
import functools
import math

import jax
import jax.numpy as jnp
from jax import lax
from jax.experimental import pallas as pl
from jax.experimental.pallas import tpu as pltpu
from jax.sharding import PartitionSpec as P

f32 = jnp.float32
bf16 = jnp.bfloat16


def dot(a, b):
    return lax.dot_general(a, b, (((1,), (0,)), ((), ())), preferred_element_type=f32)


def dot_nt(a, b):
    return lax.dot_general(a, b, (((1,), (1,)), ((), ())), preferred_element_type=f32)


def cat(parts, axis):
    return jnp.concatenate(parts, axis)


def split(x):
    hi = x.astype(bf16)
    return hi, (x - hi.astype(f32)).astype(bf16)


def product(a, b):
    n = b[0].shape[1]
    row = cat(b, 1)
    r = dot(cat(a, 1), cat([row, row], 0))
    return r[:, :n] + r[:, n:]


def odd(x, s):
    return cat([x[b * s:(b + 1) * s] for b in range(1, x.shape[0] // s, 2)], 0)


def weave(even, o, s):
    out = []
    for b in range(o.shape[0] // s):
        out.append(jnp.zeros((s, o.shape[1]), o.dtype) if even is None else even[2 * b * s:(2 * b + 1) * s])
        out.append(o[b * s:(b + 1) * s])
    return cat(out, 0)


def block_masks(C):
    i = lax.broadcasted_iota(jnp.int32, (C, C), 0)
    j = lax.broadcasted_iota(jnp.int32, (C, C), 1)
    masks = {}
    s = BASE
    while s < C:
        masks[s] = (((i // (2 * s)) == (j // (2 * s))) & ((i // s) != (j // s))).astype(bf16)
        s *= 2
    return masks, (i == j).astype(f32)


BASE = 16


def base_inverses(A):
    C = A[0].shape[0]
    i = lax.broadcasted_iota(jnp.int32, (C, C), 0)
    j = lax.broadcasted_iota(jnp.int32, (C, C), 1)
    place = (j // BASE - i // BASE) & (C // BASE - 1)
    first = j & ~(BASE - 1)
    zero = jnp.zeros((C, C), f32)
    halves = lambda x: [x.reshape(C // BASE, BASE, C)[:, r:r + 8] for r in (0, 8)]
    packs = []
    for at in range(0, len(A), C // BASE):
        packed = zero
        for p, a in enumerate(A[at:at + C // BASE]):
            packed = jnp.where(place == p, pltpu.roll(a, BASE * p, 1) if p else a, packed)
        packs.append(packed)
    start = halves(((j & (BASE - 1)) == (i & (BASE - 1))).astype(f32))
    X = [list(start) for _ in packs]
    for k in range(BASE - 1):
        for x, packed in zip(X, packs):
            lo, hi = halves(jnp.take_along_axis(packed, first + k, axis=1))
            row = x[k // 8][:, k % 8:k % 8 + 1]
            if k < 7:
                x[0] = x[0] - lo * row
            x[1] = x[1] - hi * row
    out = []
    for x, at in zip(X, range(0, len(A), C // BASE)):
        whole = jnp.concatenate(x, axis=1).reshape(C, C)
        for p in range(min(len(A) - at, C // BASE)):
            out.append(jnp.where(place == 0, pltpu.roll(whole, C - BASE * p, 1) if p else whole, zero))
    return out


def inverses(A, masks, eye):
    C = eye.shape[0]
    As = [split(a) for a in A]
    X = base_inverses(A)
    Xs = [split(x) for x in X]
    yield
    s = BASE
    while s < C:
        m = odd(masks[s], s)
        B = [split(product((odd(a[0], s) * m, odd(a[1], s) * m), x)) for a, x in zip(As, Xs)]
        B = [(weave(None, b[0], s), weave(None, b[1], s)) for b in B]
        yield
        Xo = [odd(x, s) - product((odd(xs[0], s), odd(xs[1], s)), b) for x, xs, b in zip(X, Xs, B)]
        X = [weave(x, o, s) for x, o in zip(X, Xo)]
        if 2 * s < C:
            So = [split(o) for o in Xo]
            Xs = [(weave(x[0], o[0], s), weave(x[1], o[1], s)) for x, o in zip(Xs, So)]
        yield
        s *= 2
    return X


def staggered(runs, lag):
    done = [None] * len(runs)
    t = 0
    while any(d is None for d in done):
        for i, run in enumerate(runs):
            if done[i] is None and t >= i * lag:
                try:
                    next(run)
                except StopIteration as stop:
                    done[i] = stop.value
        t += 1
    return done


def two(parts):
    x = cat(parts, 0)
    return cat([x, x], 1)


def factors(kq, k, q, v, Lr, Lc, br, bc, Lq, masks, eye):
    C, d = k[0].shape
    T = q[0].shape[0]
    H = range(len(k))
    i = lax.broadcasted_iota(jnp.int32, (C + T, C), 0)
    j = lax.broadcasted_iota(jnp.int32, (C + T, C), 1)
    visible = j <= jnp.where(i < C, i - 1, 2 * (i - C) + 1)
    nil = jnp.zeros((C, d), bf16)
    G = []
    for p, both in enumerate(kq):
        a, b = k[2 * p], k[2 * p + 1]
        r = dot_nt(both, cat([cat([a, nil], 1), cat([nil, b], 1)], 0))
        G += [r[:, :C], r[:, C:]]
    yield
    Gd = [G[h][:C] * eye for h in H]
    nr = [lax.rsqrt(jnp.sum(Gd[h], axis=0, keepdims=True) + 1e-6) for h in H]
    nc = [lax.rsqrt(jnp.sum(Gd[h], axis=1, keepdims=True) + 1e-6) for h in H]
    qn = [lax.rsqrt(jnp.sum(jnp.square(q[h].astype(f32)), axis=1, keepdims=True) + 1e-6) for h in H]
    lev = [cat([Lc[h], Lq[h]], 0) for h in H]
    rs = [cat([bc[h] * nc[h] * nc[h], qn[h]], 0) for h in H]
    M = [jnp.where(visible, jnp.exp(jnp.minimum(lev[h] - Lr[h], 0.0)) * G[h] * rs[h], 0.0) for h in H]
    yield
    X = yield from inverses([M[h][:C] for h in H], masks, eye)
    bn = [br[h] * nr[h] for h in H]
    W = [dot(cat(split(X[h] * bn[h]), 1), cat([v[h], v[h]], 0)) for h in H]
    U = [dot(cat(split(X[h] * (bn[h] * nr[h] * jnp.exp(Lr[h]))), 1), cat([k[h], k[h]], 0)) for h in H]
    yield
    last = [Lr[h][:, C - 1:C] for h in H]
    kt = [split(jnp.transpose(k[h].astype(f32)) * jnp.exp(last[h] - Lr[h])) for h in H]
    ws = [split(M[h][C:]) for h in H]
    right = [split(cat([U[h], W[h]], 1)) for h in H]
    R = [dot(two([kt[h][0], ws[h][0], kt[h][1], ws[h][1]]), cat(right[h], 0)) for h in H]
    R = [r[:d + T] + r[d + T:] for r in R]
    yield
    left = [split(cat([R[h][:d, :d], (qn[h] * jnp.exp(Lq[h])) * q[h].astype(f32) - R[h][d:, :d]], 0)) for h in H]
    return left, [R[h][:, d:] for h in H], [jnp.exp(last[h]) for h in H]


def advance(Y, left, add, decay):
    H = range(len(Y))
    d = Y[0].shape[0]
    n = left[0][0].shape[0]
    R = [dot(two(left[h]), cat(split(Y[h]), 0)) for h in H]
    R = [r[:n] + r[n:] for r in R]
    nil = jnp.zeros_like(add[0])
    own = [cat([a, nil], 1) for a in add]
    return [Y[h] * decay[h] + own[h][:d] - R[h][:d] for h in H], [own[h][d:] + R[h][d:] for h in H]


D = 128
LOCAL = 1
LIMIT = 40
BATCH = 8
LAG = 2


def params(mib):
    return pltpu.CompilerParams(vmem_limit_bytes=mib * 2**20)


def cost(us):
    return pl.CostEstimate(flops=int(us * 10**9), bytes_accessed=10**6, transcendentals=0)


def levels_body(x_ref, r_ref, *, T):
    C = 2 * T
    heads = x_ref.shape[0] // 3

    def pick(x, m):
        a = x.astype(bf16)
        r = dot(cat([a, *split(x - a.astype(f32))], 0), m.astype(bf16))
        return r[:heads] + r[heads:2 * heads] + r[2 * heads:]

    def full(x):
        return x if heads == 8 else cat([x, jnp.zeros((8 - heads, C), f32)], 0)

    b0, b1, ld = (x_ref[r * heads:(r + 1) * heads] for r in range(3))
    t = lax.broadcasted_iota(jnp.int32, (x_ref.shape[1], C), 0)
    i = lax.broadcasted_iota(jnp.int32, (x_ref.shape[1], C), 1)
    for s in range(r_ref.shape[0]):
        u = t - s * T
        r_ref[s, 0:8] = full(pick(ld, (u >= 0) & (u <= i // 2)))
        r_ref[s, 8:16] = full(pick(b0, 2 * u == i) + pick(b1, 2 * u + 1 == i))
        r_ref[s, 16:24] = full(pick(ld, (u >= 0) & (u <= i)))


def local_body(*refs, HB, NC, first, start, fresh, last):
    refs = list(refs)
    q_ref, k_ref, v_ref = refs[:3]
    y_ref = refs.pop()
    c = pl.program_id(0)
    T = q_ref.shape[0] // NC
    C = 2 * T
    d = D
    H = range(HB)
    if fresh:
        o_ref, qe_ref, r_ref, *out = refs[4:]
    else:
        r_ref, *more = refs[3:]
        if start:
            o_ref, qe_ref, *out = more[3:]
        else:
            o_ref, qe_ref, *out = more

    @pl.when(c == 0)
    def _():
        if fresh:
            levels_body(refs[3], r_ref, T=T)
        if start:
            y_ref[...] = more[0][...]
        else:
            i = lax.broadcasted_iota(jnp.int32, (d, 2 * d), 0)
            j = lax.broadcasted_iota(jnp.int32, (d, 2 * d), 1)
            for h in H:
                y_ref[h] = (j == i + d).astype(f32)

    masks, eye = block_masks(C)
    kq, k, q, v, Lr, Lc, br, bc, Lq = ([] for _ in range(9))
    for s in range(NC):
        rows = r_ref[start + c * NC + s]
        cols = jnp.transpose(cat([rows, jnp.zeros((C - 24, C), f32)], 0))
        ks = k_ref[s * T:(s + 1) * T].reshape(C, HB * d)
        vs = v_ref[s * T:(s + 1) * T].reshape(C, HB * d)
        qs = q_ref[s * T:(s + 1) * T]
        both = cat([ks, qs], 0)
        kq += [both[:, p * d:(p + 2) * d] for p in range(0, HB, 2)]
        for h in H:
            at = first + h
            k.append(ks[:, h * d:(h + 1) * d])
            v.append(vs[:, h * d:(h + 1) * d])
            q.append(qs[:, h * d:(h + 1) * d])
            Lr.append(rows[at:at + 1])
            br.append(rows[8 + at:9 + at])
            Lc.append(cols[:, at:at + 1])
            bc.append(cols[:, 8 + at:9 + at])
            Lq.append(cols[:T, 16 + at:17 + at])
    runs = []
    for at in range(0, len(k), BATCH):
        now = slice(at, at + BATCH)
        runs.append(factors(kq[at // 2:(at + BATCH) // 2], *(x[now] for x in (k, q, v, Lr, Lc, br, bc, Lq)), masks, eye))
    left, add, decay = (sum(x, []) for x in zip(*staggered(runs, LAG)))
    Y = [y_ref[h] for h in H]
    for s in range(NC):
        now = slice(s * HB, (s + 1) * HB)
        Y, o = advance(Y, left[now], add[now], decay[now])
        for h in H:
            o_ref[s * T:(s + 1) * T, h * d:(h + 1) * d] = o[h][:, :d]
            qe_ref[s * T:(s + 1) * T, h * d:(h + 1) * d] = o[h][:, d:].astype(bf16)
    for h in H:
        y_ref[h] = Y[h]

    @pl.when(c == pl.num_programs(0) - 1)
    def _():
        for h in H:
            out[0][h] = Y[h]
            if last:
                out[1][h] = Y[h].astype(bf16)
                out[2][h] = Y[h][:, :d].astype(bf16)


def local(queries, keys, values, small, g, HB, start, stop, held=(), T=64):
    n, w = queries.shape
    wg = HB * D
    NC = math.gcd(16 // HB, stop - start)
    B = NC * T
    at = start // NC
    fresh, last = small.ndim == 2, stop == n // T
    flat = pl.BlockSpec((B, wg), lambda c: (at + c, g))
    pair = pl.BlockSpec((B, 2, wg), lambda c: (at + c, 0, g))
    out = pl.BlockSpec((B, wg), lambda c: (at + c, 0))
    whole = lambda *s: pl.BlockSpec(s, lambda c: (0,) * len(s))
    rows = (n // T, 24, 2 * T)
    any_ = pl.BlockSpec(memory_space=pl.ANY)
    outs = [(out, (n, wg), f32), (out, (n, wg), bf16)]
    if fresh:
        outs.append((whole(*rows), rows, f32))
    outs.append((whole(HB, D, 2 * D), (HB, D, 2 * D), f32))
    if last:
        outs += [(whole(HB, D, 2 * D), (HB, D, 2 * D), bf16), (whole(HB, D, D), (HB, D, D), bf16)]
    return pl.pallas_call(
        functools.partial(local_body, HB=HB, NC=NC, first=g * HB, start=start, fresh=fresh, last=last),
        grid=((stop - start) // NC,),
        in_specs=[flat, pair, pair, whole(*small.shape), *([whole(HB, D, 2 * D), any_, any_] if held else [])],
        out_specs=[x[0] for x in outs],
        out_shape=[jax.ShapeDtypeStruct(x[1], x[2]) for x in outs],
        input_output_aliases={5: 0, 6: 1} if held else {},
        scratch_shapes=[pltpu.VMEM((HB, D, 2 * D), f32)],
        cost_estimate=cost(HB * LOCAL), name="local", compiler_params=params(LIMIT),
    )(queries, keys, values, small, *held)


VMEM = pl.BlockSpec(memory_space=pltpu.VMEM)


def meet_body(am_ref, a_ref, z_ref):
    for h in range(z_ref.shape[0]):
        z_ref[h] = (am_ref[h, :, :D].astype(f32) + dot(am_ref[h, :, D:], a_ref[h])).astype(bf16)


def meet(am, a):
    return pl.pallas_call(
        meet_body, in_specs=[VMEM, VMEM], out_specs=VMEM, out_shape=jax.ShapeDtypeStruct(a.shape, bf16),
        cost_estimate=cost(0.3), name="meet", compiler_params=params(8))(am, a)


def hop_body(y_ref, z_ref, out_ref):
    for h in range(y_ref.shape[0]):
        hi, lo = split(y_ref[h, :, D:])
        z = z_ref[h]
        out_ref[h] = (y_ref[h, :, :D] + dot(cat([hi, lo], 1), cat([z, z], 0))).astype(bf16)


def hop(y, z):
    return pl.pallas_call(
        hop_body, in_specs=[VMEM, VMEM], out_specs=VMEM, out_shape=jax.ShapeDtypeStruct(z.shape, bf16),
        cost_estimate=cost(0.3), name="hop", compiler_params=params(8))(y, z)


def leave_body(o_ref, qe_ref, y_ref, z_ref, out_ref):
    n = o_ref.shape[0]
    for h in range(z_ref.shape[0]):
        s = slice(h * D, h * D + D)
        z = z_ref[h]
        hi, lo = split(y_ref[h, :, D:])
        out_ref[:n, s] = (o_ref[:, s] + dot(qe_ref[:, s], z)).astype(bf16)
        out_ref[n:, s] = (y_ref[h, :, :D] + dot(cat([hi, lo], 1), cat([z, z], 0))).astype(bf16)


def leave(o, qe, y, z):
    n, w = o.shape
    return pl.pallas_call(
        leave_body, in_specs=[VMEM] * 4, out_specs=VMEM, out_shape=jax.ShapeDtypeStruct((n + D, w), bf16),
        cost_estimate=cost(0.5), name="leave", compiler_params=params(8))(o, qe, y, z)


def weigh_body(q_ref, kp_ref, ko_ref, p_ref, *, axis, R, first):
    n = q_ref.shape[0]
    h = pl.program_id(0)
    bias = jnp.where(lax.axis_index(axis) > 0, 0.0, -1e30).astype(f32)
    scale = D ** -0.5 * math.log2(math.e)
    tri = lax.broadcasted_iota(jnp.int32, (R, R), 1) <= lax.broadcasted_iota(jnp.int32, (R, R), 0)
    kp = kp_ref[:, pl.ds(pl.multiple_of((first + h) * D, D), D)]
    for i in range(n // R):
        q = q_ref[i * R:(i + 1) * R]
        sp = dot_nt(q, kp) + bias
        so = dot_nt(q, ko_ref[:(i + 1) * R])
        diag = jnp.where(tri, so[:, i * R:], -1e30)
        so = diag if i == 0 else cat([so[:, :i * R], diag], 1)
        m = jnp.maximum(jnp.max(sp, 1, keepdims=True), jnp.max(so, 1, keepdims=True))
        ep = jnp.exp2((sp - m) * scale)
        eo = jnp.exp2((so - m) * scale)
        inv = 1.0 / (jnp.sum(ep, 1, keepdims=True) + jnp.sum(eo, 1, keepdims=True))
        p_ref[0, i * R:(i + 1) * R, :n] = (ep * inv).astype(bf16)
        p_ref[0, i * R:(i + 1) * R, n:n + (i + 1) * R] = (eo * inv).astype(bf16)
        if (i + 1) * R < n:
            p_ref[0, i * R:(i + 1) * R, n + (i + 1) * R:] = jnp.zeros((R, n - (i + 1) * R), bf16)


def weigh(q, kp, ko, g, HB, R=256, axis="ctx"):
    n, w = q.shape
    flat = pl.BlockSpec((n, D), lambda h: (0, g * HB + h))
    return pl.pallas_call(
        functools.partial(weigh_body, axis=axis, R=R, first=g * HB), grid=(HB,),
        in_specs=[flat, VMEM, flat], out_specs=pl.BlockSpec((1, n, 2 * n), lambda h: (h, 0, 0)),
        out_shape=jax.ShapeDtypeStruct((HB, n, 2 * n), bf16),
        cost_estimate=cost(HB * 1.3), name="weigh", compiler_params=params(24))(q, kp, ko)


def gather_body(o_ref, qe_ref, p_ref, vz_ref, *refs):
    ret_ref, out_ref = refs[-2:]
    n = o_ref.shape[0]
    vz = vz_ref[:, pl.ds(pl.multiple_of(pl.program_id(0) * D, D), D)]
    ret = (o_ref[...] + dot(qe_ref[...], vz[n:])).astype(bf16)
    ret_ref[...] = ret
    out_ref[...] = dot(p_ref[pl.program_id(0)], cat([vz[:n], ret], 0)).astype(bf16)


def gather(o, qe, p, vz, carry, g, HB, w):
    n = o.shape[0]
    part = pl.BlockSpec((n, D), lambda h: (0, h))
    flat = pl.BlockSpec((n, D), lambda h: (0, g * HB + h))
    held = [pl.BlockSpec(memory_space=pl.ANY)] * len(carry)
    return pl.pallas_call(
        gather_body, grid=(HB,), in_specs=[part, part, VMEM, VMEM] + held,
        out_specs=[flat, flat], out_shape=[jax.ShapeDtypeStruct((n, w), bf16)] * 2,
        input_output_aliases={4 + i: i for i in range(len(carry))},
        cost_estimate=cost(HB * 0.5), name="gather", compiler_params=params(24))(o, qe, p, vz, *carry)


def send(array, pairs):
    return lax.ppermute(array, "ctx", pairs) if pairs else jnp.zeros_like(array)


def per_device(queries, keys, values, betas, log_decay, attn_queries, attn_keys):
    n, w = queries.shape
    HB = w // D // 2
    chunks = n // 64
    blocks = lax.axis_size("ctx")
    every = [(i, i + 1) for i in range(blocks - 1)]
    keys_behind = send(attn_keys, every)

    def pass_on(o, qe, y, near, far):
        z = meet(near, far)
        for k in range(3, blocks - 1):
            z = z + send(hop(y, z), [(k - 1, k)])
        return leave(o, qe, y, z)

    def round_one(am, a):
        far = send(a, [(0, 2)] if blocks > 2 else [])
        return send(am, every[:2]), far

    small = cat([betas[:, 0], betas[:, 1], log_decay], 1).transpose(1, 0)
    o0, qe0, rows, y0, am, a = local(queries, keys, values, small, 0, HB, 0, chunks)
    near, far = round_one(am, a)
    o1, qe1, y1 = local(queries, keys, values, rows, 1, HB, 0, chunks // 2)
    near, far, y1 = lax.optimization_barrier((near, far, y1))
    leaving = pass_on(o0, qe0, y0, near, far)
    leaving, y1 = lax.optimization_barrier((leaving, y1))
    crossing0 = send(leaving, every)
    o1, qe1, y1, am, a = local(queries, keys, values, rows, 1, HB, chunks // 2, chunks, (y1, o1, qe1))
    near, far = round_one(am, a)
    keys_behind, y1 = lax.optimization_barrier((keys_behind, y1))
    weights = [weigh(attn_queries, keys_behind, attn_keys, 0, HB)]
    keys_behind, crossing0, weights = lax.optimization_barrier((keys_behind, crossing0, weights))
    weights.append(weigh(attn_queries, keys_behind, attn_keys, 1, HB))
    near, far, weights = lax.optimization_barrier((near, far, weights))
    crossing1 = send(pass_on(o1, qe1, y1, near, far), every)
    done = gather(o0, qe0, weights[0], crossing0, (), 0, HB, w)
    return tuple(gather(o1, qe1, weights[1], crossing1, tuple(done), 1, HB, w))


def solution(mesh):
    rows, cols = ("groups", "ctx"), ("head", "sub")
    flat, paired = P(rows, cols), P(rows, None, cols)
    return jax.shard_map(
        per_device,
        mesh=mesh,
        in_specs=(flat, paired, paired, paired, flat, flat, flat),
        out_specs=(flat, flat),
        check_vma=False,
    )
```

```python
import functools
import math

import jax
import jax.numpy as jnp
from jax import lax
from jax.experimental import pallas as pl
from jax.experimental.pallas import tpu as pltpu
from jax.sharding import PartitionSpec as P

f32 = jnp.float32
bf16 = jnp.bfloat16


def dot(a, b):
    return lax.dot_general(a, b, (((1,), (0,)), ((), ())), preferred_element_type=f32)


def dot_nt(a, b):
    return lax.dot_general(a, b, (((1,), (1,)), ((), ())), preferred_element_type=f32)


def cat(parts, axis):
    return jnp.concatenate(parts, axis)


def split(x):
    hi = x.astype(bf16)
    return hi, (x - hi.astype(f32)).astype(bf16)


def product(a, b):
    n = b[0].shape[1]
    row = cat(b, 1)
    r = dot(cat(a, 1), cat([row, row], 0))
    return r[:, :n] + r[:, n:]


def odd(x, s):
    return cat([x[b * s:(b + 1) * s] for b in range(1, x.shape[0] // s, 2)], 0)


def weave(even, o, s):
    out = []
    for b in range(o.shape[0] // s):
        out.append(jnp.zeros((s, o.shape[1]), o.dtype) if even is None else even[2 * b * s:(2 * b + 1) * s])
        out.append(o[b * s:(b + 1) * s])
    return cat(out, 0)


def block_masks(C):
    i = lax.broadcasted_iota(jnp.int32, (C, C), 0)
    j = lax.broadcasted_iota(jnp.int32, (C, C), 1)
    masks = {}
    s = BASE
    while s < C:
        masks[s] = (((i // (2 * s)) == (j // (2 * s))) & ((i // s) != (j // s))).astype(bf16)
        s *= 2
    return masks, (i == j).astype(f32)


BASE = 16


def base_inverses(A):
    C = A[0].shape[0]
    i = lax.broadcasted_iota(jnp.int32, (C, C), 0)
    j = lax.broadcasted_iota(jnp.int32, (C, C), 1)
    place = (j // BASE - i // BASE) & (C // BASE - 1)
    first = j & ~(BASE - 1)
    zero = jnp.zeros((C, C), f32)
    halves = lambda x: [x.reshape(C // BASE, BASE, C)[:, r:r + 8] for r in (0, 8)]
    packs = []
    for at in range(0, len(A), C // BASE):
        packed = zero
        for p, a in enumerate(A[at:at + C // BASE]):
            packed = jnp.where(place == p, pltpu.roll(a, BASE * p, 1) if p else a, packed)
        packs.append(packed)
    start = halves(((j & (BASE - 1)) == (i & (BASE - 1))).astype(f32))
    X = [list(start) for _ in packs]
    for k in range(BASE - 1):
        for x, packed in zip(X, packs):
            lo, hi = halves(jnp.take_along_axis(packed, first + k, axis=1))
            row = x[k // 8][:, k % 8:k % 8 + 1]
            if k < 7:
                x[0] = x[0] - lo * row
            x[1] = x[1] - hi * row
    out = []
    for x, at in zip(X, range(0, len(A), C // BASE)):
        whole = jnp.concatenate(x, axis=1).reshape(C, C)
        for p in range(min(len(A) - at, C // BASE)):
            out.append(jnp.where(place == 0, pltpu.roll(whole, C - BASE * p, 1) if p else whole, zero))
    return out


def inverses(A, masks, eye):
    C = eye.shape[0]
    As = [split(a) for a in A]
    X = base_inverses(A)
    Xs = [split(x) for x in X]
    yield
    s = BASE
    while s < C:
        m = odd(masks[s], s)
        B = [split(product((odd(a[0], s) * m, odd(a[1], s) * m), x)) for a, x in zip(As, Xs)]
        B = [(weave(None, b[0], s), weave(None, b[1], s)) for b in B]
        yield
        Xo = [odd(x, s) - product((odd(xs[0], s), odd(xs[1], s)), b) for x, xs, b in zip(X, Xs, B)]
        X = [weave(x, o, s) for x, o in zip(X, Xo)]
        if 2 * s < C:
            So = [split(o) for o in Xo]
            Xs = [(weave(x[0], o[0], s), weave(x[1], o[1], s)) for x, o in zip(Xs, So)]
        yield
        s *= 2
    return X


def staggered(runs, lag):
    done = [None] * len(runs)
    t = 0
    while any(d is None for d in done):
        for i, run in enumerate(runs):
            if done[i] is None and t >= i * lag:
                try:
                    next(run)
                except StopIteration as stop:
                    done[i] = stop.value
        t += 1
    return done


def two(parts):
    x = cat(parts, 0)
    return cat([x, x], 1)


def factors(kq, k, q, v, Lr, Lc, br, bc, Lq, masks, eye):
    C, d = k[0].shape
    T = q[0].shape[0]
    H = range(len(k))
    i = lax.broadcasted_iota(jnp.int32, (C + T, C), 0)
    j = lax.broadcasted_iota(jnp.int32, (C + T, C), 1)
    visible = j <= jnp.where(i < C, i - 1, 2 * (i - C) + 1)
    nil = jnp.zeros((C, d), bf16)
    G = []
    for p, both in enumerate(kq):
        a, b = k[2 * p], k[2 * p + 1]
        r = dot_nt(both, cat([cat([a, nil], 1), cat([nil, b], 1)], 0))
        G += [r[:, :C], r[:, C:]]
    yield
    Gd = [G[h][:C] * eye for h in H]
    nr = [lax.rsqrt(jnp.sum(Gd[h], axis=0, keepdims=True) + 1e-6) for h in H]
    nc = [lax.rsqrt(jnp.sum(Gd[h], axis=1, keepdims=True) + 1e-6) for h in H]
    qn = [lax.rsqrt(jnp.sum(jnp.square(q[h].astype(f32)), axis=1, keepdims=True) + 1e-6) for h in H]
    lev = [cat([Lc[h], Lq[h]], 0) for h in H]
    rs = [cat([bc[h] * nc[h] * nc[h], qn[h]], 0) for h in H]
    M = [jnp.where(visible, jnp.exp(jnp.minimum(lev[h] - Lr[h], 0.0)) * G[h] * rs[h], 0.0) for h in H]
    yield
    X = yield from inverses([M[h][:C] for h in H], masks, eye)
    bn = [br[h] * nr[h] for h in H]
    W = [dot(cat(split(X[h] * bn[h]), 1), cat([v[h], v[h]], 0)) for h in H]
    U = [dot(cat(split(X[h] * (bn[h] * nr[h] * jnp.exp(Lr[h]))), 1), cat([k[h], k[h]], 0)) for h in H]
    yield
    last = [Lr[h][:, C - 1:C] for h in H]
    kt = [split(jnp.transpose(k[h].astype(f32)) * jnp.exp(last[h] - Lr[h])) for h in H]
    ws = [split(M[h][C:]) for h in H]
    right = [split(cat([U[h], W[h]], 1)) for h in H]
    R = [dot(two([kt[h][0], ws[h][0], kt[h][1], ws[h][1]]), cat(right[h], 0)) for h in H]
    R = [r[:d + T] + r[d + T:] for r in R]
    yield
    left = [split(cat([R[h][:d, :d], (qn[h] * jnp.exp(Lq[h])) * q[h].astype(f32) - R[h][d:, :d]], 0)) for h in H]
    return left, [R[h][:, d:] for h in H], [jnp.exp(last[h]) for h in H]


def advance(Y, left, add, decay):
    H = range(len(Y))
    d = Y[0].shape[0]
    n = left[0][0].shape[0]
    R = [dot(two(left[h]), cat(split(Y[h]), 0)) for h in H]
    R = [r[:n] + r[n:] for r in R]
    nil = jnp.zeros_like(add[0])
    own = [cat([a, nil], 1) for a in add]
    return [Y[h] * decay[h] + own[h][:d] - R[h][:d] for h in H], [own[h][d:] + R[h][d:] for h in H]


D = 128
LOCAL = 1
LIMIT = 24
FIRST = 48
BATCH = 8
LAG = 2
STEP = 2


def params(mib):
    return pltpu.CompilerParams(vmem_limit_bytes=mib * 2**20)


def cost(us):
    return pl.CostEstimate(flops=int(us * 10**9), bytes_accessed=10**6, transcendentals=0)


def levels_body(x_ref, r_ref, *, T):
    C = 2 * T
    heads = x_ref.shape[0] // 3

    def pick(x, m):
        a = x.astype(bf16)
        r = dot(cat([a, *split(x - a.astype(f32))], 0), m.astype(bf16))
        return r[:heads] + r[heads:2 * heads] + r[2 * heads:]

    def full(x):
        return x if heads == 8 else cat([x, jnp.zeros((8 - heads, C), f32)], 0)

    b0, b1, ld = (x_ref[r * heads:(r + 1) * heads] for r in range(3))
    t = lax.broadcasted_iota(jnp.int32, (x_ref.shape[1], C), 0)
    i = lax.broadcasted_iota(jnp.int32, (x_ref.shape[1], C), 1)
    for s in range(r_ref.shape[0]):
        u = t - s * T
        r_ref[s, 0:8] = full(pick(ld, (u >= 0) & (u <= i // 2)))
        r_ref[s, 8:16] = full(pick(b0, 2 * u == i) + pick(b1, 2 * u + 1 == i))
        r_ref[s, 16:24] = full(pick(ld, (u >= 0) & (u <= i)))


VMEM = pl.BlockSpec(memory_space=pltpu.VMEM)


def run_chunks(keys, queries, values, r_ref, y_ref, o_ref, qe_ref, HB, NC, first, chunk_at, out_at):
    C = keys.shape[0] // NC
    T = C // 2
    d = D
    H = range(HB)
    masks, eye = block_masks(C)
    kq, k, q, v, Lr, Lc, br, bc, Lq = ([] for _ in range(9))
    for s in range(NC):
        rows = r_ref[chunk_at + s]
        cols = jnp.transpose(cat([rows, jnp.zeros((C - 24, C), f32)], 0))
        ks = keys[s * C:(s + 1) * C]
        vs = values[s * C:(s + 1) * C]
        qs = queries[s * T:(s + 1) * T]
        both = cat([ks, qs], 0)
        kq += [both[:, p * d:(p + 2) * d] for p in range(0, HB, 2)]
        for h in H:
            at = first + h
            k.append(ks[:, h * d:(h + 1) * d])
            v.append(vs[:, h * d:(h + 1) * d])
            q.append(qs[:, h * d:(h + 1) * d])
            Lr.append(rows[at:at + 1])
            br.append(rows[8 + at:9 + at])
            Lc.append(cols[:, at:at + 1])
            bc.append(cols[:, 8 + at:9 + at])
            Lq.append(cols[:T, 16 + at:17 + at])
    runs = []
    for at in range(0, len(k), BATCH):
        now = slice(at, at + BATCH)
        runs.append(factors(kq[at // 2:(at + BATCH) // 2], *(x[now] for x in (k, q, v, Lr, Lc, br, bc, Lq)), masks, eye))
    left, add, decay = (sum(x, []) for x in zip(*staggered(runs, LAG)))
    Y = [y_ref[h] for h in H]
    for s in range(NC):
        now = slice(s * HB, (s + 1) * HB)
        Y, o = advance(Y, left[now], add[now], decay[now])
        for h in H:
            rows = pl.ds(out_at + s * T, T)
            o_ref[rows, h * d:(h + 1) * d] = o[h][:, :d]
            qe_ref[rows, h * d:(h + 1) * d] = o[h][:, d:].astype(bf16)
    for h in H:
        y_ref[h] = Y[h]
    return Y


def put(Y, refs):
    for h, y in enumerate(Y):
        refs[0][h] = y
        refs[1][h] = y.astype(bf16)
        refs[2][h] = y[:, :D].astype(bf16)


def open_body(q_ref, k_ref, v_ref, x_ref, o_ref, qe_ref, r_ref, qk_ref, kk_ref, vk_ref, yo_ref, am_ref, a_ref, y_ref, *, HB, NC):
    c = pl.program_id(0)
    T = q_ref.shape[0] // NC
    wg = HB * D

    @pl.when(c == 0)
    def _():
        levels_body(x_ref, r_ref, T=T)
        i = lax.broadcasted_iota(jnp.int32, (D, 2 * D), 0)
        j = lax.broadcasted_iota(jnp.int32, (D, 2 * D), 1)
        for h in range(HB):
            y_ref[h] = (j == i + D).astype(f32)

    flat = lambda ref, at: ref[:, :, at:at + wg].reshape(2 * NC * T, wg)
    here = pl.multiple_of(c * NC * T, NC * T)
    double = pl.multiple_of(2 * c * NC * T, 2 * NC * T)
    qk_ref[pl.ds(here, NC * T)] = q_ref[:, wg:]
    kk_ref[pl.ds(double, 2 * NC * T)] = flat(k_ref, wg)
    vk_ref[pl.ds(double, 2 * NC * T)] = flat(v_ref, wg)
    Y = run_chunks(flat(k_ref, 0), q_ref[:, :wg], flat(v_ref, 0), r_ref, y_ref, o_ref, qe_ref, HB, NC, 0, c * NC, 0)

    @pl.when(c == pl.num_programs(0) - 1)
    def _():
        put(Y, (yo_ref, am_ref, a_ref))


def local_open(queries, keys, values, small, HB, T=64):
    n, w = queries.shape
    wg = HB * D
    NC = math.gcd(16 // HB, n // T)
    B = NC * T
    flat = pl.BlockSpec((B, w), lambda c: (c, 0))
    pair = pl.BlockSpec((B, 2, w), lambda c: (c, 0, 0))
    out = pl.BlockSpec((B, wg), lambda c: (c, 0))
    whole = lambda *s: pl.BlockSpec(s, lambda c: (0,) * len(s))
    rows, state = (n // T, 24, 2 * T), (HB, D, 2 * D)
    outs = [
        (out, (n, wg), f32), (out, (n, wg), bf16), (whole(*rows), rows, f32),
        (VMEM, (n, wg), bf16), (VMEM, (2 * n, wg), bf16), (VMEM, (2 * n, wg), bf16),
        (whole(*state), state, f32), (whole(*state), state, bf16), (whole(HB, D, D), (HB, D, D), bf16),
    ]
    return pl.pallas_call(
        functools.partial(open_body, HB=HB, NC=NC), grid=(n // B,),
        in_specs=[flat, pair, pair, whole(*small.shape)],
        out_specs=[x[0] for x in outs], out_shape=[jax.ShapeDtypeStruct(x[1], x[2]) for x in outs],
        scratch_shapes=[pltpu.VMEM(state, f32)],
        cost_estimate=cost(HB * LOCAL), name="local_open", compiler_params=params(FIRST),
    )(queries, keys, values, small)


def half_body(q_ref, k_ref, v_ref, r_ref, *refs, HB, NC, start):
    n = q_ref.shape[0]
    T = 64
    if start:
        y_in, o_ref, qe_ref, yo_ref, am_ref, a_ref, y_ref = refs
        y_ref[...] = y_in[...]
    else:
        o_ref, qe_ref, yo_ref, y_ref = refs
        i = lax.broadcasted_iota(jnp.int32, (D, 2 * D), 0)
        j = lax.broadcasted_iota(jnp.int32, (D, 2 * D), 1)
        for h in range(HB):
            y_ref[h] = (j == i + D).astype(f32)
    for s in range(0, o_ref.shape[0] // T, NC):
        at = start + s
        token, double = slice(at * T, (at + NC) * T), slice(2 * at * T, 2 * (at + NC) * T)
        Y = run_chunks(k_ref[double], q_ref[token], v_ref[double], r_ref, y_ref, o_ref, qe_ref, HB, NC, HB, at, s * T)
    if start:
        put(Y, (yo_ref, am_ref, a_ref))
    else:
        yo_ref[...] = y_ref[...]


def local_half(q, k, v, rows, HB, start, stop, state=None, T=64):
    n, wg = q.shape
    m = (stop - start) * T
    shape = (HB, D, 2 * D)
    outs = [((m, wg), f32), ((m, wg), bf16), (shape, f32)]
    if start:
        outs += [(shape, bf16), ((HB, D, D), bf16)]
    args = (q, k, v, rows) + ((state,) if start else ())
    return pl.pallas_call(
        functools.partial(half_body, HB=HB, NC=math.gcd(16 // HB, stop - start), start=start),
        in_specs=[VMEM] * len(args), out_specs=[VMEM] * len(outs), out_shape=[jax.ShapeDtypeStruct(*x) for x in outs],
        scratch_shapes=[pltpu.VMEM(shape, f32)],
        cost_estimate=cost(HB * LOCAL), name="local_half", compiler_params=params(LIMIT),
    )(*args)


def meet_body(am_ref, a_ref, z_ref):
    for h in range(z_ref.shape[0]):
        z_ref[h] = (am_ref[h, :, :D].astype(f32) + dot(am_ref[h, :, D:], a_ref[h])).astype(bf16)


def meet(am, a):
    return pl.pallas_call(
        meet_body, in_specs=[VMEM, VMEM], out_specs=VMEM, out_shape=jax.ShapeDtypeStruct(a.shape, bf16),
        cost_estimate=cost(0.3), name="meet", compiler_params=params(8))(am, a)


def hop_body(y_ref, z_ref, out_ref):
    for h in range(y_ref.shape[0]):
        hi, lo = split(y_ref[h, :, D:])
        z = z_ref[h]
        out_ref[h] = (y_ref[h, :, :D] + dot(cat([hi, lo], 1), cat([z, z], 0))).astype(bf16)


def hop(y, z):
    return pl.pallas_call(
        hop_body, in_specs=[VMEM, VMEM], out_specs=VMEM, out_shape=jax.ShapeDtypeStruct(z.shape, bf16),
        cost_estimate=cost(0.3), name="hop", compiler_params=params(8))(y, z)


def leave_body(*refs):
    parts, (y_ref, z_ref, out_ref) = refs[:-3], refs[-3:]
    at = 0
    for o_ref, qe_ref in zip(parts[::2], parts[1::2]):
        m = o_ref.shape[0]
        for h in range(z_ref.shape[0]):
            s = slice(h * D, h * D + D)
            out_ref[at:at + m, s] = (o_ref[:, s] + dot(qe_ref[:, s], z_ref[h])).astype(bf16)
        at += m
    for h in range(z_ref.shape[0]):
        z = z_ref[h]
        hi, lo = split(y_ref[h, :, D:])
        out_ref[at:, h * D:h * D + D] = (y_ref[h, :, :D] + dot(cat([hi, lo], 1), cat([z, z], 0))).astype(bf16)


def leave(parts, y, z):
    n = sum(x[0].shape[0] for x in parts)
    args = [x for p in parts for x in p] + [y, z]
    return pl.pallas_call(
        leave_body, in_specs=[VMEM] * len(args), out_specs=VMEM, out_shape=jax.ShapeDtypeStruct((n + D, y.shape[0] * D), bf16),
        cost_estimate=cost(0.5), name="leave", compiler_params=params(8))(*args)


def weigh_body(q_ref, kp_ref, ko_ref, p_ref, *, axis, R, first):
    n = q_ref.shape[0]
    h = pl.program_id(0)
    bias = jnp.where(lax.axis_index(axis) > 0, 0.0, -1e30).astype(f32)
    scale = D ** -0.5 * math.log2(math.e)
    tri = lax.broadcasted_iota(jnp.int32, (R, R), 1) <= lax.broadcasted_iota(jnp.int32, (R, R), 0)
    kp = kp_ref[:, pl.ds(pl.multiple_of((first + h) * D, D), D)]
    for i in range(n // R):
        q = q_ref[i * R:(i + 1) * R]
        sp = dot_nt(q, kp) + bias
        so = dot_nt(q, ko_ref[:(i + 1) * R])
        diag = jnp.where(tri, so[:, i * R:], -1e30)
        so = diag if i == 0 else cat([so[:, :i * R], diag], 1)
        m = jnp.maximum(jnp.max(sp, 1, keepdims=True), jnp.max(so, 1, keepdims=True))
        ep = jnp.exp2((sp - m) * scale)
        eo = jnp.exp2((so - m) * scale)
        inv = 1.0 / (jnp.sum(ep, 1, keepdims=True) + jnp.sum(eo, 1, keepdims=True))
        p_ref[0, i * R:(i + 1) * R, :n] = (ep * inv).astype(bf16)
        p_ref[0, i * R:(i + 1) * R, n:n + (i + 1) * R] = (eo * inv).astype(bf16)
        if (i + 1) * R < n:
            p_ref[0, i * R:(i + 1) * R, n + (i + 1) * R:] = jnp.zeros((R, n - (i + 1) * R), bf16)


def weigh(q, kp, ko, g, HB, R=256, axis="ctx"):
    n, w = q.shape
    flat = pl.BlockSpec((n, D), lambda h: (0, g * HB + h))
    return pl.pallas_call(
        functools.partial(weigh_body, axis=axis, R=R, first=g * HB), grid=(HB,),
        in_specs=[flat, VMEM, flat], out_specs=pl.BlockSpec((1, n, 2 * n), lambda h: (h, 0, 0)),
        out_shape=jax.ShapeDtypeStruct((HB, n, 2 * n), bf16),
        cost_estimate=cost(HB * 1.3), name="weigh", compiler_params=params(24))(q, kp, ko)


def gather_body(*refs, step, count):
    parts, (p_ref, vz_ref) = refs[:2 * count], refs[2 * count:2 * count + 2]
    ret_ref, out_ref = refs[-2:]
    n = ret_ref.shape[0]
    for h in range(step):
        s = slice(h * D, h * D + D)
        vz = vz_ref[:, pl.ds(pl.multiple_of((pl.program_id(0) * step + h) * D, D), D)]
        ret = cat([(o[:, s] + dot(qe[:, s], vz[n:])).astype(bf16) for o, qe in zip(parts[::2], parts[1::2])], 0)
        ret_ref[:, s] = ret
        out_ref[:, s] = dot(p_ref[pl.program_id(0) * step + h], cat([vz[:n], ret], 0)).astype(bf16)


def gather(parts, p, vz, carry, g, HB, w):
    n = p.shape[1]
    step = math.gcd(STEP, HB)
    args = [x for pair in parts for x in pair]
    flat = pl.BlockSpec((n, step * D), lambda h: (0, g * (HB // step) + h))
    held = [pl.BlockSpec(memory_space=pl.ANY)] * len(carry)
    return pl.pallas_call(
        functools.partial(gather_body, step=step, count=len(parts)), grid=(HB // step,),
        in_specs=[pl.BlockSpec((x.shape[0], step * D), lambda h: (0, h)) for x in args] + [VMEM, VMEM] + held,
        out_specs=[flat, flat], out_shape=[jax.ShapeDtypeStruct((n, w), bf16)] * 2,
        input_output_aliases={len(args) + 2 + i: i for i in range(len(carry))},
        cost_estimate=cost(HB * 0.5), name="gather", compiler_params=params(24))(*args, p, vz, *carry)


def send(array, pairs):
    return lax.ppermute(array, "ctx", pairs) if pairs else jnp.zeros_like(array)


def per_device(queries, keys, values, betas, log_decay, attn_queries, attn_keys):
    n, w = queries.shape
    HB = w // D // 2
    chunks = n // 64
    blocks = lax.axis_size("ctx")
    every = [(i, i + 1) for i in range(blocks - 1)]
    keys_behind = send(attn_keys, every)

    def pass_on(parts, y, near, far):
        z = meet(near, far)
        for k in range(3, blocks - 1):
            z = z + send(hop(y, z), [(k - 1, k)])
        return leave(parts, y, z)

    def round_one(am, a):
        far = send(a, [(0, 2)] if blocks > 2 else [])
        return send(am, every[:2]), far

    small = cat([betas[:, 0], betas[:, 1], log_decay], 1).transpose(1, 0)
    o0, qe0, rows, q1, k1, v1, y0, am, a = local_open(queries, keys, values, small, HB)
    near, far = round_one(am, a)
    first = ((o0, qe0),)
    oa, qa, y1 = local_half(q1, k1, v1, rows, HB, 0, chunks // 2)
    near, far, y1 = lax.optimization_barrier((near, far, y1))
    leaving = pass_on(first, y0, near, far)
    leaving, y1 = lax.optimization_barrier((leaving, y1))
    crossing0 = send(leaving, every)
    ob, qb, y1, am, a = local_half(q1, k1, v1, rows, HB, chunks // 2, chunks, y1)
    second = ((oa, qa), (ob, qb))
    near, far = round_one(am, a)
    keys_behind, y1 = lax.optimization_barrier((keys_behind, y1))
    weights = [weigh(attn_queries, keys_behind, attn_keys, 0, HB)]
    keys_behind, crossing0, weights = lax.optimization_barrier((keys_behind, crossing0, weights))
    weights.append(weigh(attn_queries, keys_behind, attn_keys, 1, HB))
    near, far, weights = lax.optimization_barrier((near, far, weights))
    crossing1 = send(pass_on(second, y1, near, far), every)
    done = gather(first, weights[0], crossing0, (), 0, HB, w)
    return tuple(gather(second, weights[1], crossing1, tuple(done), 1, HB, w))


def solution(mesh):
    rows, cols = ("groups", "ctx"), ("head", "sub")
    flat, paired = P(rows, cols), P(rows, None, cols)
    return jax.shard_map(
        per_device,
        mesh=mesh,
        in_specs=(flat, paired, paired, paired, flat, flat, flat),
        out_specs=(flat, flat),
        check_vma=False,
    )
```

```python
import functools
import math

import jax
import jax.numpy as jnp
from jax import lax
from jax.experimental import pallas as pl
from jax.experimental.pallas import tpu as pltpu
from jax.sharding import PartitionSpec as P

f32 = jnp.float32
bf16 = jnp.bfloat16


def dot(a, b):
    return lax.dot_general(a, b, (((1,), (0,)), ((), ())), preferred_element_type=f32)


def dot_nt(a, b):
    return lax.dot_general(a, b, (((1,), (1,)), ((), ())), preferred_element_type=f32)


def cat(parts, axis):
    return jnp.concatenate(parts, axis)


def split(x):
    hi = x.astype(bf16)
    return hi, (x - hi.astype(f32)).astype(bf16)


def product(a, b):
    n = b[0].shape[1]
    row = cat(b, 1)
    r = dot(cat(a, 1), cat([row, row], 0))
    return r[:, :n] + r[:, n:]


def odd(x, s):
    return cat([x[b * s:(b + 1) * s] for b in range(1, x.shape[0] // s, 2)], 0)


def weave(even, o, s):
    out = []
    for b in range(o.shape[0] // s):
        out.append(jnp.zeros((s, o.shape[1]), o.dtype) if even is None else even[2 * b * s:(2 * b + 1) * s])
        out.append(o[b * s:(b + 1) * s])
    return cat(out, 0)


def block_masks(C):
    i = lax.broadcasted_iota(jnp.int32, (C, C), 0)
    j = lax.broadcasted_iota(jnp.int32, (C, C), 1)
    masks = {}
    s = BASE
    while s < C:
        masks[s] = (((i // (2 * s)) == (j // (2 * s))) & ((i // s) != (j // s))).astype(bf16)
        s *= 2
    return masks, (i == j).astype(f32)


BASE = 16


def base_inverses(A):
    C = A[0].shape[0]
    i = lax.broadcasted_iota(jnp.int32, (C, C), 0)
    j = lax.broadcasted_iota(jnp.int32, (C, C), 1)
    place = (j // BASE - i // BASE) & (C // BASE - 1)
    first = j & ~(BASE - 1)
    zero = jnp.zeros((C, C), f32)
    halves = lambda x: [x.reshape(C // BASE, BASE, C)[:, r:r + 8] for r in (0, 8)]
    packs = []
    for at in range(0, len(A), C // BASE):
        packed = zero
        for p, a in enumerate(A[at:at + C // BASE]):
            packed = jnp.where(place == p, pltpu.roll(a, BASE * p, 1) if p else a, packed)
        packs.append(packed)
    start = halves(((j & (BASE - 1)) == (i & (BASE - 1))).astype(f32))
    X = [list(start) for _ in packs]
    for k in range(BASE - 1):
        for x, packed in zip(X, packs):
            lo, hi = halves(jnp.take_along_axis(packed, first + k, axis=1))
            row = x[k // 8][:, k % 8:k % 8 + 1]
            if k < 7:
                x[0] = x[0] - lo * row
            x[1] = x[1] - hi * row
    out = []
    for x, at in zip(X, range(0, len(A), C // BASE)):
        whole = jnp.concatenate(x, axis=1).reshape(C, C)
        for p in range(min(len(A) - at, C // BASE)):
            out.append(jnp.where(place == 0, pltpu.roll(whole, C - BASE * p, 1) if p else whole, zero))
    return out


def inverses(A, masks, eye):
    C = eye.shape[0]
    As = [split(a) for a in A]
    X = base_inverses(A)
    Xs = [split(x) for x in X]
    yield
    s = BASE
    while s < C:
        m = odd(masks[s], s)
        B = [split(product((odd(a[0], s) * m, odd(a[1], s) * m), x)) for a, x in zip(As, Xs)]
        B = [(weave(None, b[0], s), weave(None, b[1], s)) for b in B]
        yield
        Xo = [odd(x, s) - product((odd(xs[0], s), odd(xs[1], s)), b) for x, xs, b in zip(X, Xs, B)]
        X = [weave(x, o, s) for x, o in zip(X, Xo)]
        if 2 * s < C:
            So = [split(o) for o in Xo]
            Xs = [(weave(x[0], o[0], s), weave(x[1], o[1], s)) for x, o in zip(Xs, So)]
        yield
        s *= 2
    return X


def staggered(runs, lag):
    done = [None] * len(runs)
    t = 0
    while any(d is None for d in done):
        for i, run in enumerate(runs):
            if done[i] is None and t >= i * lag:
                try:
                    next(run)
                except StopIteration as stop:
                    done[i] = stop.value
        t += 1
    return done


def two(parts):
    x = cat(parts, 0)
    return cat([x, x], 1)


def factors(kq, k, q, v, Lr, Lc, br, bc, Lq, masks, eye):
    C, d = k[0].shape
    T = q[0].shape[0]
    H = range(len(k))
    i = lax.broadcasted_iota(jnp.int32, (C + T, C), 0)
    j = lax.broadcasted_iota(jnp.int32, (C + T, C), 1)
    visible = j <= jnp.where(i < C, i - 1, 2 * (i - C) + 1)
    nil = jnp.zeros((C, d), bf16)
    G = []
    for p, both in enumerate(kq):
        a, b = k[2 * p], k[2 * p + 1]
        r = dot_nt(both, cat([cat([a, nil], 1), cat([nil, b], 1)], 0))
        G += [r[:, :C], r[:, C:]]
    yield
    Gd = [G[h][:C] * eye for h in H]
    nr = [lax.rsqrt(jnp.sum(Gd[h], axis=0, keepdims=True) + 1e-6) for h in H]
    nc = [lax.rsqrt(jnp.sum(Gd[h], axis=1, keepdims=True) + 1e-6) for h in H]
    qn = [lax.rsqrt(jnp.sum(jnp.square(q[h].astype(f32)), axis=1, keepdims=True) + 1e-6) for h in H]
    lev = [cat([Lc[h], Lq[h]], 0) for h in H]
    rs = [cat([bc[h] * nc[h] * nc[h], qn[h]], 0) for h in H]
    M = [jnp.where(visible, jnp.exp(jnp.minimum(lev[h] - Lr[h], 0.0)) * G[h] * rs[h], 0.0) for h in H]
    yield
    X = yield from inverses([M[h][:C] for h in H], masks, eye)
    bn = [br[h] * nr[h] for h in H]
    W = [dot(cat(split(X[h] * bn[h]), 1), cat([v[h], v[h]], 0)) for h in H]
    U = [dot(cat(split(X[h] * (bn[h] * nr[h] * jnp.exp(Lr[h]))), 1), cat([k[h], k[h]], 0)) for h in H]
    yield
    last = [Lr[h][:, C - 1:C] for h in H]
    kt = [split(jnp.transpose(k[h].astype(f32)) * jnp.exp(last[h] - Lr[h])) for h in H]
    ws = [split(M[h][C:]) for h in H]
    right = [split(cat([U[h], W[h]], 1)) for h in H]
    R = [dot(two([kt[h][0], ws[h][0], kt[h][1], ws[h][1]]), cat(right[h], 0)) for h in H]
    R = [r[:d + T] + r[d + T:] for r in R]
    yield
    left = [split(cat([R[h][:d, :d], (qn[h] * jnp.exp(Lq[h])) * q[h].astype(f32) - R[h][d:, :d]], 0)) for h in H]
    return left, [R[h][:, d:] for h in H], [jnp.exp(last[h]) for h in H]


def advance(Y, left, add, decay):
    H = range(len(Y))
    d = Y[0].shape[0]
    n = left[0][0].shape[0]
    R = [dot(two(left[h]), cat(split(Y[h]), 0)) for h in H]
    R = [r[:n] + r[n:] for r in R]
    nil = jnp.zeros_like(add[0])
    own = [cat([a, nil], 1) for a in add]
    return [Y[h] * decay[h] + own[h][:d] - R[h][:d] for h in H], [own[h][d:] + R[h][d:] for h in H]


D = 128
LOCAL = 1
LIMIT = 24
FIRST = 48
BATCH = 8
LAG = 2
STEP = 4


def params(mib):
    return pltpu.CompilerParams(vmem_limit_bytes=mib * 2**20)


def cost(us):
    return pl.CostEstimate(flops=int(us * 10**9), bytes_accessed=10**6, transcendentals=0)


def levels_body(x_ref, r_ref, *, T):
    C = 2 * T
    heads = x_ref.shape[0] // 3

    def pick(x, m):
        a = x.astype(bf16)
        r = dot(cat([a, *split(x - a.astype(f32))], 0), m.astype(bf16))
        return r[:heads] + r[heads:2 * heads] + r[2 * heads:]

    def full(x):
        return x if heads == 8 else cat([x, jnp.zeros((8 - heads, C), f32)], 0)

    b0, b1, ld = (x_ref[r * heads:(r + 1) * heads] for r in range(3))
    t = lax.broadcasted_iota(jnp.int32, (x_ref.shape[1], C), 0)
    i = lax.broadcasted_iota(jnp.int32, (x_ref.shape[1], C), 1)
    for s in range(r_ref.shape[0]):
        u = t - s * T
        r_ref[s, 0:8] = full(pick(ld, (u >= 0) & (u <= i // 2)))
        r_ref[s, 8:16] = full(pick(b0, 2 * u == i) + pick(b1, 2 * u + 1 == i))
        r_ref[s, 16:24] = full(pick(ld, (u >= 0) & (u <= i)))


VMEM = pl.BlockSpec(memory_space=pltpu.VMEM)


def run_chunks(keys, queries, values, r_ref, y_ref, o_ref, qe_ref, HB, NC, first, chunk_at, out_at):
    C = keys.shape[0] // NC
    T = C // 2
    d = D
    H = range(HB)
    masks, eye = block_masks(C)
    kq, k, q, v, Lr, Lc, br, bc, Lq = ([] for _ in range(9))
    for s in range(NC):
        rows = r_ref[chunk_at + s]
        cols = jnp.transpose(cat([rows, jnp.zeros((C - 24, C), f32)], 0))
        ks = keys[s * C:(s + 1) * C]
        vs = values[s * C:(s + 1) * C]
        qs = queries[s * T:(s + 1) * T]
        both = cat([ks, qs], 0)
        kq += [both[:, p * d:(p + 2) * d] for p in range(0, HB, 2)]
        for h in H:
            at = first + h
            k.append(ks[:, h * d:(h + 1) * d])
            v.append(vs[:, h * d:(h + 1) * d])
            q.append(qs[:, h * d:(h + 1) * d])
            Lr.append(rows[at:at + 1])
            br.append(rows[8 + at:9 + at])
            Lc.append(cols[:, at:at + 1])
            bc.append(cols[:, 8 + at:9 + at])
            Lq.append(cols[:T, 16 + at:17 + at])
    runs = []
    for at in range(0, len(k), BATCH):
        now = slice(at, at + BATCH)
        runs.append(factors(kq[at // 2:(at + BATCH) // 2], *(x[now] for x in (k, q, v, Lr, Lc, br, bc, Lq)), masks, eye))
    left, add, decay = (sum(x, []) for x in zip(*staggered(runs, LAG)))
    Y = [y_ref[h] for h in H]
    for s in range(NC):
        now = slice(s * HB, (s + 1) * HB)
        Y, o = advance(Y, left[now], add[now], decay[now])
        for h in H:
            rows = pl.ds(out_at + s * T, T)
            o_ref[rows, h * d:(h + 1) * d] = o[h][:, :d]
            qe_ref[rows, h * d:(h + 1) * d] = o[h][:, d:].astype(bf16)
    for h in H:
        y_ref[h] = Y[h]
    return Y


def put(Y, refs):
    for h, y in enumerate(Y):
        refs[0][h] = y
        refs[1][h] = y.astype(bf16)
        refs[2][h] = y[:, :D].astype(bf16)


def open_body(q_ref, k_ref, v_ref, x_ref, o_ref, qe_ref, r_ref, qk_ref, kk_ref, vk_ref, yo_ref, am_ref, a_ref, y_ref, *, HB, NC):
    c = pl.program_id(0)
    T = q_ref.shape[0] // NC
    wg = HB * D

    @pl.when(c == 0)
    def _():
        levels_body(x_ref, r_ref, T=T)
        i = lax.broadcasted_iota(jnp.int32, (D, 2 * D), 0)
        j = lax.broadcasted_iota(jnp.int32, (D, 2 * D), 1)
        for h in range(HB):
            y_ref[h] = (j == i + D).astype(f32)

    flat = lambda ref, at: ref[:, :, at:at + wg].reshape(2 * NC * T, wg)
    here = pl.multiple_of(c * NC * T, NC * T)
    double = pl.multiple_of(2 * c * NC * T, 2 * NC * T)
    qk_ref[pl.ds(here, NC * T)] = q_ref[:, wg:]
    kk_ref[pl.ds(double, 2 * NC * T)] = flat(k_ref, wg)
    vk_ref[pl.ds(double, 2 * NC * T)] = flat(v_ref, wg)
    Y = run_chunks(flat(k_ref, 0), q_ref[:, :wg], flat(v_ref, 0), r_ref, y_ref, o_ref, qe_ref, HB, NC, 0, c * NC, 0)

    @pl.when(c == pl.num_programs(0) - 1)
    def _():
        put(Y, (yo_ref, am_ref, a_ref))


def local_open(queries, keys, values, small, HB, T=64):
    n, w = queries.shape
    wg = HB * D
    NC = math.gcd(16 // HB, n // T)
    B = NC * T
    flat = pl.BlockSpec((B, w), lambda c: (c, 0))
    pair = pl.BlockSpec((B, 2, w), lambda c: (c, 0, 0))
    out = pl.BlockSpec((B, wg), lambda c: (c, 0))
    whole = lambda *s: pl.BlockSpec(s, lambda c: (0,) * len(s))
    rows, state = (n // T, 24, 2 * T), (HB, D, 2 * D)
    outs = [
        (out, (n, wg), f32), (out, (n, wg), bf16), (whole(*rows), rows, f32),
        (VMEM, (n, wg), bf16), (VMEM, (2 * n, wg), bf16), (VMEM, (2 * n, wg), bf16),
        (whole(*state), state, f32), (whole(*state), state, bf16), (whole(HB, D, D), (HB, D, D), bf16),
    ]
    return pl.pallas_call(
        functools.partial(open_body, HB=HB, NC=NC), grid=(n // B,),
        in_specs=[flat, pair, pair, whole(*small.shape)],
        out_specs=[x[0] for x in outs], out_shape=[jax.ShapeDtypeStruct(x[1], x[2]) for x in outs],
        scratch_shapes=[pltpu.VMEM(state, f32)],
        cost_estimate=cost(HB * LOCAL), name="local_open", compiler_params=params(FIRST),
    )(queries, keys, values, small)


def half_body(q_ref, k_ref, v_ref, r_ref, *refs, HB, NC, start):
    n = q_ref.shape[0]
    T = 64
    if start:
        y_in, o_ref, qe_ref, yo_ref, am_ref, a_ref, y_ref = refs
        y_ref[...] = y_in[...]
    else:
        o_ref, qe_ref, yo_ref, y_ref = refs
        i = lax.broadcasted_iota(jnp.int32, (D, 2 * D), 0)
        j = lax.broadcasted_iota(jnp.int32, (D, 2 * D), 1)
        for h in range(HB):
            y_ref[h] = (j == i + D).astype(f32)
    for s in range(0, o_ref.shape[0] // T, NC):
        at = start + s
        token, double = slice(at * T, (at + NC) * T), slice(2 * at * T, 2 * (at + NC) * T)
        Y = run_chunks(k_ref[double], q_ref[token], v_ref[double], r_ref, y_ref, o_ref, qe_ref, HB, NC, HB, at, s * T)
    if start:
        put(Y, (yo_ref, am_ref, a_ref))
    else:
        yo_ref[...] = y_ref[...]


def local_half(q, k, v, rows, HB, start, stop, state=None, T=64):
    n, wg = q.shape
    m = (stop - start) * T
    shape = (HB, D, 2 * D)
    outs = [((m, wg), f32), ((m, wg), bf16), (shape, f32)]
    if start:
        outs += [(shape, bf16), ((HB, D, D), bf16)]
    args = (q, k, v, rows) + ((state,) if start else ())
    return pl.pallas_call(
        functools.partial(half_body, HB=HB, NC=math.gcd(16 // HB, stop - start), start=start),
        in_specs=[VMEM] * len(args), out_specs=[VMEM] * len(outs), out_shape=[jax.ShapeDtypeStruct(*x) for x in outs],
        scratch_shapes=[pltpu.VMEM(shape, f32)],
        cost_estimate=cost(HB * LOCAL), name="local_half", compiler_params=params(LIMIT),
    )(*args)


def meet_body(am_ref, a_ref, z_ref):
    for h in range(z_ref.shape[0]):
        z_ref[h] = (am_ref[h, :, :D].astype(f32) + dot(am_ref[h, :, D:], a_ref[h])).astype(bf16)


def meet(am, a):
    return pl.pallas_call(
        meet_body, in_specs=[VMEM, VMEM], out_specs=VMEM, out_shape=jax.ShapeDtypeStruct(a.shape, bf16),
        cost_estimate=cost(0.3), name="meet", compiler_params=params(8))(am, a)


def hop_body(y_ref, z_ref, out_ref):
    for h in range(y_ref.shape[0]):
        hi, lo = split(y_ref[h, :, D:])
        z = z_ref[h]
        out_ref[h] = (y_ref[h, :, :D] + dot(cat([hi, lo], 1), cat([z, z], 0))).astype(bf16)


def hop(y, z):
    return pl.pallas_call(
        hop_body, in_specs=[VMEM, VMEM], out_specs=VMEM, out_shape=jax.ShapeDtypeStruct(z.shape, bf16),
        cost_estimate=cost(0.3), name="hop", compiler_params=params(8))(y, z)


def leave_body(*refs):
    parts, (y_ref, z_ref, out_ref) = refs[:-3], refs[-3:]
    at = 0
    for o_ref, qe_ref in zip(parts[::2], parts[1::2]):
        m = o_ref.shape[0]
        for h in range(z_ref.shape[0]):
            s = slice(h * D, h * D + D)
            out_ref[at:at + m, s] = (o_ref[:, s] + dot(qe_ref[:, s], z_ref[h])).astype(bf16)
        at += m
    for h in range(z_ref.shape[0]):
        z = z_ref[h]
        hi, lo = split(y_ref[h, :, D:])
        out_ref[at:, h * D:h * D + D] = (y_ref[h, :, :D] + dot(cat([hi, lo], 1), cat([z, z], 0))).astype(bf16)


def leave(parts, y, z):
    n = sum(x[0].shape[0] for x in parts)
    args = [x for p in parts for x in p] + [y, z]
    return pl.pallas_call(
        leave_body, in_specs=[VMEM] * len(args), out_specs=VMEM, out_shape=jax.ShapeDtypeStruct((n + D, y.shape[0] * D), bf16),
        cost_estimate=cost(0.5), name="leave", compiler_params=params(8))(*args)


def weigh_body(q_ref, kp_ref, ko_ref, p_ref, *, axis, R, first):
    n = q_ref.shape[0]
    h = pl.program_id(0)
    bias = jnp.where(lax.axis_index(axis) > 0, 0.0, -1e30).astype(f32)
    scale = D ** -0.5 * math.log2(math.e)
    tri = lax.broadcasted_iota(jnp.int32, (R, R), 1) <= lax.broadcasted_iota(jnp.int32, (R, R), 0)
    kp = kp_ref[:, pl.ds(pl.multiple_of((first + h) * D, D), D)]
    for i in range(n // R):
        q = q_ref[i * R:(i + 1) * R]
        sp = dot_nt(q, kp) + bias
        so = dot_nt(q, ko_ref[:(i + 1) * R])
        diag = jnp.where(tri, so[:, i * R:], -1e30)
        so = diag if i == 0 else cat([so[:, :i * R], diag], 1)
        m = jnp.maximum(jnp.max(sp, 1, keepdims=True), jnp.max(so, 1, keepdims=True))
        ep = jnp.exp2((sp - m) * scale)
        eo = jnp.exp2((so - m) * scale)
        inv = 1.0 / (jnp.sum(ep, 1, keepdims=True) + jnp.sum(eo, 1, keepdims=True))
        p_ref[0, i * R:(i + 1) * R, :n] = (ep * inv).astype(bf16)
        p_ref[0, i * R:(i + 1) * R, n:n + (i + 1) * R] = (eo * inv).astype(bf16)
        if (i + 1) * R < n:
            p_ref[0, i * R:(i + 1) * R, n + (i + 1) * R:] = jnp.zeros((R, n - (i + 1) * R), bf16)


def weigh(q, kp, ko, g, HB, R=256, axis="ctx"):
    n, w = q.shape
    flat = pl.BlockSpec((n, D), lambda h: (0, g * HB + h))
    return pl.pallas_call(
        functools.partial(weigh_body, axis=axis, R=R, first=g * HB), grid=(HB,),
        in_specs=[flat, VMEM, flat], out_specs=pl.BlockSpec((1, n, 2 * n), lambda h: (h, 0, 0)),
        out_shape=jax.ShapeDtypeStruct((HB, n, 2 * n), bf16),
        cost_estimate=cost(HB * 1.3), name="weigh", compiler_params=params(24))(q, kp, ko)


def gather_body(*refs, step, count):
    parts, (p_ref, vz_ref) = refs[:2 * count], refs[2 * count:2 * count + 2]
    ret_ref, out_ref = refs[-2:]
    n = ret_ref.shape[0]
    for h in range(step):
        s = slice(h * D, h * D + D)
        vz = vz_ref[:, pl.ds(pl.multiple_of((pl.program_id(0) * step + h) * D, D), D)]
        mine = pl.ds(pl.multiple_of((pl.program_id(0) * step + h) * D, D), D)
        ret = cat([(o[:, mine] + dot(qe[:, mine], vz[n:])).astype(bf16) for o, qe in zip(parts[::2], parts[1::2])], 0)
        ret_ref[:, s] = ret
        out_ref[:, s] = dot(p_ref[pl.program_id(0) * step + h], cat([vz[:n], ret], 0)).astype(bf16)


def gather(parts, p, vz, carry, g, HB, w):
    n = p.shape[1]
    step = math.gcd(STEP, HB)
    args = [x for pair in parts for x in pair]
    flat = pl.BlockSpec((n, step * D), lambda h: (0, g * (HB // step) + h))
    held = [pl.BlockSpec(memory_space=pl.ANY)] * len(carry)
    return pl.pallas_call(
        functools.partial(gather_body, step=step, count=len(parts)), grid=(HB // step,),
        in_specs=[VMEM] * (len(args) + 2) + held,
        out_specs=[flat, flat], out_shape=[jax.ShapeDtypeStruct((n, w), bf16)] * 2,
        input_output_aliases={len(args) + 2 + i: i for i in range(len(carry))},
        cost_estimate=cost(HB * 0.5), name="gather", compiler_params=params(24))(*args, p, vz, *carry)


def send(array, pairs):
    return lax.ppermute(array, "ctx", pairs) if pairs else jnp.zeros_like(array)


def per_device(queries, keys, values, betas, log_decay, attn_queries, attn_keys):
    n, w = queries.shape
    HB = w // D // 2
    chunks = n // 64
    blocks = lax.axis_size("ctx")
    every = [(i, i + 1) for i in range(blocks - 1)]
    keys_behind = send(attn_keys, every)

    def pass_on(parts, y, near, far):
        z = meet(near, far)
        for k in range(3, blocks - 1):
            z = z + send(hop(y, z), [(k - 1, k)])
        return leave(parts, y, z)

    def round_one(am, a):
        far = send(a, [(0, 2)] if blocks > 2 else [])
        return send(am, every[:2]), far

    small = cat([betas[:, 0], betas[:, 1], log_decay], 1).transpose(1, 0)
    o0, qe0, rows, q1, k1, v1, y0, am, a = local_open(queries, keys, values, small, HB)
    near, far = round_one(am, a)
    first = ((o0, qe0),)
    oa, qa, y1 = local_half(q1, k1, v1, rows, HB, 0, chunks // 2)
    near, far, y1 = lax.optimization_barrier((near, far, y1))
    leaving = pass_on(first, y0, near, far)
    leaving, y1 = lax.optimization_barrier((leaving, y1))
    crossing0 = send(leaving, every)
    ob, qb, y1, am, a = local_half(q1, k1, v1, rows, HB, chunks // 2, chunks, y1)
    second = ((oa, qa), (ob, qb))
    near, far = round_one(am, a)
    keys_behind, y1 = lax.optimization_barrier((keys_behind, y1))
    weights = [weigh(attn_queries, keys_behind, attn_keys, 0, HB)]
    keys_behind, crossing0, weights = lax.optimization_barrier((keys_behind, crossing0, weights))
    weights.append(weigh(attn_queries, keys_behind, attn_keys, 1, HB))
    near, far, weights = lax.optimization_barrier((near, far, weights))
    crossing1 = send(pass_on(second, y1, near, far), every)
    done = gather(first, weights[0], crossing0, (), 0, HB, w)
    return tuple(gather(second, weights[1], crossing1, tuple(done), 1, HB, w))


def solution(mesh):
    rows, cols = ("groups", "ctx"), ("head", "sub")
    flat, paired = P(rows, cols), P(rows, None, cols)
    return jax.shard_map(
        per_device,
        mesh=mesh,
        in_specs=(flat, paired, paired, paired, flat, flat, flat),
        out_specs=(flat, flat),
        check_vma=False,
    )
```

```python
import functools
import math

import jax
import jax.numpy as jnp
from jax import lax
from jax.experimental import pallas as pl
from jax.experimental.pallas import tpu as pltpu
from jax.sharding import PartitionSpec as P

f32 = jnp.float32
bf16 = jnp.bfloat16


def dot(a, b):
    return lax.dot_general(a, b, (((1,), (0,)), ((), ())), preferred_element_type=f32)


def dot_nt(a, b):
    return lax.dot_general(a, b, (((1,), (1,)), ((), ())), preferred_element_type=f32)


def cat(parts, axis):
    return jnp.concatenate(parts, axis)


def split(x):
    hi = x.astype(bf16)
    return hi, (x - hi.astype(f32)).astype(bf16)


def product(a, b):
    n = b[0].shape[1]
    row = cat(b, 1)
    r = dot(cat(a, 1), cat([row, row], 0))
    return r[:, :n] + r[:, n:]


def odd(x, s):
    return cat([x[b * s:(b + 1) * s] for b in range(1, x.shape[0] // s, 2)], 0)


def weave(even, o, s):
    out = []
    for b in range(o.shape[0] // s):
        out.append(jnp.zeros((s, o.shape[1]), o.dtype) if even is None else even[2 * b * s:(2 * b + 1) * s])
        out.append(o[b * s:(b + 1) * s])
    return cat(out, 0)


def block_masks(C):
    i = lax.broadcasted_iota(jnp.int32, (C, C), 0)
    j = lax.broadcasted_iota(jnp.int32, (C, C), 1)
    masks = {}
    s = BASE
    while s < C:
        masks[s] = (((i // (2 * s)) == (j // (2 * s))) & ((i // s) != (j // s))).astype(bf16)
        s *= 2
    return masks, (i == j).astype(f32)


BASE = 16


def base_inverses(A):
    C = A[0].shape[0]
    i = lax.broadcasted_iota(jnp.int32, (C, C), 0)
    j = lax.broadcasted_iota(jnp.int32, (C, C), 1)
    place = (j // BASE - i // BASE) & (C // BASE - 1)
    first = j & ~(BASE - 1)
    zero = jnp.zeros((C, C), f32)
    halves = lambda x: [x.reshape(C // BASE, BASE, C)[:, r:r + 8] for r in (0, 8)]
    packs = []
    for at in range(0, len(A), C // BASE):
        packed = zero
        for p, a in enumerate(A[at:at + C // BASE]):
            packed = jnp.where(place == p, pltpu.roll(a, BASE * p, 1) if p else a, packed)
        packs.append(packed)
    start = halves(((j & (BASE - 1)) == (i & (BASE - 1))).astype(f32))
    X = [list(start) for _ in packs]
    for k in range(BASE - 1):
        for x, packed in zip(X, packs):
            lo, hi = halves(jnp.take_along_axis(packed, first + k, axis=1))
            row = x[k // 8][:, k % 8:k % 8 + 1]
            if k < 7:
                x[0] = x[0] - lo * row
            x[1] = x[1] - hi * row
    out = []
    for x, at in zip(X, range(0, len(A), C // BASE)):
        whole = jnp.concatenate(x, axis=1).reshape(C, C)
        for p in range(min(len(A) - at, C // BASE)):
            out.append(jnp.where(place == 0, pltpu.roll(whole, C - BASE * p, 1) if p else whole, zero))
    return out


def inverses(A, masks, eye):
    C = eye.shape[0]
    As = [split(a) for a in A]
    X = base_inverses(A)
    Xs = [split(x) for x in X]
    yield
    s = BASE
    while s < C:
        m = odd(masks[s], s)
        B = [split(product((odd(a[0], s) * m, odd(a[1], s) * m), x)) for a, x in zip(As, Xs)]
        B = [(weave(None, b[0], s), weave(None, b[1], s)) for b in B]
        yield
        Xo = [odd(x, s) - product((odd(xs[0], s), odd(xs[1], s)), b) for x, xs, b in zip(X, Xs, B)]
        X = [weave(x, o, s) for x, o in zip(X, Xo)]
        if 2 * s < C:
            So = [split(o) for o in Xo]
            Xs = [(weave(x[0], o[0], s), weave(x[1], o[1], s)) for x, o in zip(Xs, So)]
        yield
        s *= 2
    return X


def staggered(runs, lag):
    done = [None] * len(runs)
    t = 0
    while any(d is None for d in done):
        for i, run in enumerate(runs):
            if done[i] is None and t >= i * lag:
                try:
                    next(run)
                except StopIteration as stop:
                    done[i] = stop.value
        t += 1
    return done


def two(parts):
    x = cat(parts, 0)
    return cat([x, x], 1)


def factors(kq, k, q, v, Lr, Lc, br, bc, Lq, masks, eye):
    C, d = k[0].shape
    T = q[0].shape[0]
    H = range(len(k))
    i = lax.broadcasted_iota(jnp.int32, (C + T, C), 0)
    j = lax.broadcasted_iota(jnp.int32, (C + T, C), 1)
    visible = j <= jnp.where(i < C, i - 1, 2 * (i - C) + 1)
    nil = jnp.zeros((C, d), bf16)
    G = []
    for p, both in enumerate(kq):
        a, b = k[2 * p], k[2 * p + 1]
        r = dot_nt(both, cat([cat([a, nil], 1), cat([nil, b], 1)], 0))
        G += [r[:, :C], r[:, C:]]
    yield
    Gd = [G[h][:C] * eye for h in H]
    nr = [lax.rsqrt(jnp.sum(Gd[h], axis=0, keepdims=True) + 1e-6) for h in H]
    nc = [lax.rsqrt(jnp.sum(Gd[h], axis=1, keepdims=True) + 1e-6) for h in H]
    qn = [lax.rsqrt(jnp.sum(jnp.square(q[h].astype(f32)), axis=1, keepdims=True) + 1e-6) for h in H]
    lev = [cat([Lc[h], Lq[h]], 0) for h in H]
    rs = [cat([bc[h] * nc[h] * nc[h], qn[h]], 0) for h in H]
    M = [jnp.where(visible, jnp.exp(jnp.minimum(lev[h] - Lr[h], 0.0)) * G[h] * rs[h], 0.0) for h in H]
    yield
    X = yield from inverses([M[h][:C] for h in H], masks, eye)
    bn = [br[h] * nr[h] for h in H]
    W = [dot(cat(split(X[h] * bn[h]), 1), cat([v[h], v[h]], 0)) for h in H]
    U = [dot(cat(split(X[h] * (bn[h] * nr[h] * jnp.exp(Lr[h]))), 1), cat([k[h], k[h]], 0)) for h in H]
    yield
    last = [Lr[h][:, C - 1:C] for h in H]
    kt = [split(jnp.transpose(k[h].astype(f32)) * jnp.exp(last[h] - Lr[h])) for h in H]
    ws = [split(M[h][C:]) for h in H]
    right = [split(cat([U[h], W[h]], 1)) for h in H]
    R = [dot(two([kt[h][0], ws[h][0], kt[h][1], ws[h][1]]), cat(right[h], 0)) for h in H]
    R = [r[:d + T] + r[d + T:] for r in R]
    yield
    left = [split(cat([R[h][:d, :d], (qn[h] * jnp.exp(Lq[h])) * q[h].astype(f32) - R[h][d:, :d]], 0)) for h in H]
    return left, [R[h][:, d:] for h in H], [jnp.exp(last[h]) for h in H]


def advance(Y, left, add, decay):
    H = range(len(Y))
    d = Y[0].shape[0]
    n = left[0][0].shape[0]
    R = [dot(two(left[h]), cat(split(Y[h]), 0)) for h in H]
    R = [r[:n] + r[n:] for r in R]
    nil = jnp.zeros_like(add[0])
    own = [cat([a, nil], 1) for a in add]
    return [Y[h] * decay[h] + own[h][:d] - R[h][:d] for h in H], [own[h][d:] + R[h][d:] for h in H]


D = 128
LOCAL = 1
LIMIT = 24
FIRST = 48
BATCH = 8
LAG = 3
STEP = 4


def params(mib):
    return pltpu.CompilerParams(vmem_limit_bytes=mib * 2**20)


def cost(us):
    return pl.CostEstimate(flops=int(us * 10**9), bytes_accessed=10**6, transcendentals=0)


def levels_body(x_ref, r_ref, *, T):
    C = 2 * T
    heads = x_ref.shape[0] // 3

    def pick(x, m):
        a = x.astype(bf16)
        r = dot(cat([a, *split(x - a.astype(f32))], 0), m.astype(bf16))
        return r[:heads] + r[heads:2 * heads] + r[2 * heads:]

    def full(x):
        return x if heads == 8 else cat([x, jnp.zeros((8 - heads, C), f32)], 0)

    b0, b1, ld = (x_ref[r * heads:(r + 1) * heads] for r in range(3))
    t = lax.broadcasted_iota(jnp.int32, (x_ref.shape[1], C), 0)
    i = lax.broadcasted_iota(jnp.int32, (x_ref.shape[1], C), 1)
    for s in range(r_ref.shape[0]):
        u = t - s * T
        r_ref[s, 0:8] = full(pick(ld, (u >= 0) & (u <= i // 2)))
        r_ref[s, 8:16] = full(pick(b0, 2 * u == i) + pick(b1, 2 * u + 1 == i))
        r_ref[s, 16:24] = full(pick(ld, (u >= 0) & (u <= i)))


VMEM = pl.BlockSpec(memory_space=pltpu.VMEM)


def run_chunks(keys, queries, values, r_ref, y_ref, o_ref, qe_ref, HB, NC, first, chunk_at, out_at):
    C = keys.shape[0] // NC
    T = C // 2
    d = D
    H = range(HB)
    masks, eye = block_masks(C)
    kq, k, q, v, Lr, Lc, br, bc, Lq = ([] for _ in range(9))
    for s in range(NC):
        rows = r_ref[chunk_at + s]
        cols = jnp.transpose(cat([rows, jnp.zeros((C - 24, C), f32)], 0))
        ks = keys[s * C:(s + 1) * C]
        vs = values[s * C:(s + 1) * C]
        qs = queries[s * T:(s + 1) * T]
        both = cat([ks, qs], 0)
        kq += [both[:, p * d:(p + 2) * d] for p in range(0, HB, 2)]
        for h in H:
            at = first + h
            k.append(ks[:, h * d:(h + 1) * d])
            v.append(vs[:, h * d:(h + 1) * d])
            q.append(qs[:, h * d:(h + 1) * d])
            Lr.append(rows[at:at + 1])
            br.append(rows[8 + at:9 + at])
            Lc.append(cols[:, at:at + 1])
            bc.append(cols[:, 8 + at:9 + at])
            Lq.append(cols[:T, 16 + at:17 + at])
    runs = []
    for at in range(0, len(k), BATCH):
        now = slice(at, at + BATCH)
        runs.append(factors(kq[at // 2:(at + BATCH) // 2], *(x[now] for x in (k, q, v, Lr, Lc, br, bc, Lq)), masks, eye))
    left, add, decay = (sum(x, []) for x in zip(*staggered(runs, LAG)))
    Y = [y_ref[h] for h in H]
    for s in range(NC):
        now = slice(s * HB, (s + 1) * HB)
        Y, o = advance(Y, left[now], add[now], decay[now])
        for h in H:
            rows = pl.ds(out_at + s * T, T)
            o_ref[rows, h * d:(h + 1) * d] = o[h][:, :d]
            qe_ref[rows, h * d:(h + 1) * d] = o[h][:, d:].astype(bf16)
    for h in H:
        y_ref[h] = Y[h]
    return Y


def put(Y, refs):
    for h, y in enumerate(Y):
        refs[0][h] = y
        refs[1][h] = y.astype(bf16)
        refs[2][h] = y[:, :D].astype(bf16)


def open_body(q_ref, k_ref, v_ref, x_ref, o_ref, qe_ref, r_ref, qk_ref, kk_ref, vk_ref, yo_ref, am_ref, a_ref, y_ref, *, HB, NC):
    c = pl.program_id(0)
    T = q_ref.shape[0] // NC
    wg = HB * D

    @pl.when(c == 0)
    def _():
        levels_body(x_ref, r_ref, T=T)
        i = lax.broadcasted_iota(jnp.int32, (D, 2 * D), 0)
        j = lax.broadcasted_iota(jnp.int32, (D, 2 * D), 1)
        for h in range(HB):
            y_ref[h] = (j == i + D).astype(f32)

    flat = lambda ref, at: ref[:, :, at:at + wg].reshape(2 * NC * T, wg)
    here = pl.multiple_of(c * NC * T, NC * T)
    double = pl.multiple_of(2 * c * NC * T, 2 * NC * T)
    qk_ref[pl.ds(here, NC * T)] = q_ref[:, wg:]
    kk_ref[pl.ds(double, 2 * NC * T)] = flat(k_ref, wg)
    vk_ref[pl.ds(double, 2 * NC * T)] = flat(v_ref, wg)
    Y = run_chunks(flat(k_ref, 0), q_ref[:, :wg], flat(v_ref, 0), r_ref, y_ref, o_ref, qe_ref, HB, NC, 0, c * NC, 0)

    @pl.when(c == pl.num_programs(0) - 1)
    def _():
        put(Y, (yo_ref, am_ref, a_ref))


def local_open(queries, keys, values, small, HB, T=64):
    n, w = queries.shape
    wg = HB * D
    NC = math.gcd(16 // HB, n // T)
    B = NC * T
    flat = pl.BlockSpec((B, w), lambda c: (c, 0))
    pair = pl.BlockSpec((B, 2, w), lambda c: (c, 0, 0))
    out = pl.BlockSpec((B, wg), lambda c: (c, 0))
    whole = lambda *s: pl.BlockSpec(s, lambda c: (0,) * len(s))
    rows, state = (n // T, 24, 2 * T), (HB, D, 2 * D)
    outs = [
        (out, (n, wg), f32), (out, (n, wg), bf16), (whole(*rows), rows, f32),
        (VMEM, (n, wg), bf16), (VMEM, (2 * n, wg), bf16), (VMEM, (2 * n, wg), bf16),
        (whole(*state), state, f32), (whole(*state), state, bf16), (whole(HB, D, D), (HB, D, D), bf16),
    ]
    return pl.pallas_call(
        functools.partial(open_body, HB=HB, NC=NC), grid=(n // B,),
        in_specs=[flat, pair, pair, whole(*small.shape)],
        out_specs=[x[0] for x in outs], out_shape=[jax.ShapeDtypeStruct(x[1], x[2]) for x in outs],
        scratch_shapes=[pltpu.VMEM(state, f32)],
        cost_estimate=cost(HB * LOCAL), name="local_open", compiler_params=params(FIRST),
    )(queries, keys, values, small)


def half_body(q_ref, k_ref, v_ref, r_ref, *refs, HB, NC, start):
    n = q_ref.shape[0]
    T = 64
    if start:
        y_in, o_ref, qe_ref, yo_ref, am_ref, a_ref, y_ref = refs
        y_ref[...] = y_in[...]
    else:
        o_ref, qe_ref, yo_ref, y_ref = refs
        i = lax.broadcasted_iota(jnp.int32, (D, 2 * D), 0)
        j = lax.broadcasted_iota(jnp.int32, (D, 2 * D), 1)
        for h in range(HB):
            y_ref[h] = (j == i + D).astype(f32)
    for s in range(0, o_ref.shape[0] // T, NC):
        at = start + s
        token, double = slice(at * T, (at + NC) * T), slice(2 * at * T, 2 * (at + NC) * T)
        Y = run_chunks(k_ref[double], q_ref[token], v_ref[double], r_ref, y_ref, o_ref, qe_ref, HB, NC, HB, at, s * T)
    if start:
        put(Y, (yo_ref, am_ref, a_ref))
    else:
        yo_ref[...] = y_ref[...]


def local_half(q, k, v, rows, HB, start, stop, state=None, T=64):
    n, wg = q.shape
    m = (stop - start) * T
    shape = (HB, D, 2 * D)
    outs = [((m, wg), f32), ((m, wg), bf16), (shape, f32)]
    if start:
        outs += [(shape, bf16), ((HB, D, D), bf16)]
    args = (q, k, v, rows) + ((state,) if start else ())
    return pl.pallas_call(
        functools.partial(half_body, HB=HB, NC=math.gcd(16 // HB, stop - start), start=start),
        in_specs=[VMEM] * len(args), out_specs=[VMEM] * len(outs), out_shape=[jax.ShapeDtypeStruct(*x) for x in outs],
        scratch_shapes=[pltpu.VMEM(shape, f32)],
        cost_estimate=cost(HB * LOCAL), name="local_half", compiler_params=params(LIMIT),
    )(*args)


def meet_body(am_ref, a_ref, z_ref):
    for h in range(z_ref.shape[0]):
        z_ref[h] = (am_ref[h, :, :D].astype(f32) + dot(am_ref[h, :, D:], a_ref[h])).astype(bf16)


def meet(am, a):
    return pl.pallas_call(
        meet_body, in_specs=[VMEM, VMEM], out_specs=VMEM, out_shape=jax.ShapeDtypeStruct(a.shape, bf16),
        cost_estimate=cost(0.3), name="meet", compiler_params=params(8))(am, a)


def hop_body(y_ref, z_ref, out_ref):
    for h in range(y_ref.shape[0]):
        hi, lo = split(y_ref[h, :, D:])
        z = z_ref[h]
        out_ref[h] = (y_ref[h, :, :D] + dot(cat([hi, lo], 1), cat([z, z], 0))).astype(bf16)


def hop(y, z):
    return pl.pallas_call(
        hop_body, in_specs=[VMEM, VMEM], out_specs=VMEM, out_shape=jax.ShapeDtypeStruct(z.shape, bf16),
        cost_estimate=cost(0.3), name="hop", compiler_params=params(8))(y, z)


def leave_body(*refs):
    parts, (y_ref, z_ref, out_ref) = refs[:-3], refs[-3:]
    at = 0
    for o_ref, qe_ref in zip(parts[::2], parts[1::2]):
        m = o_ref.shape[0]
        for h in range(z_ref.shape[0]):
            s = slice(h * D, h * D + D)
            out_ref[at:at + m, s] = (o_ref[:, s] + dot(qe_ref[:, s], z_ref[h])).astype(bf16)
        at += m
    for h in range(z_ref.shape[0]):
        z = z_ref[h]
        hi, lo = split(y_ref[h, :, D:])
        out_ref[at:, h * D:h * D + D] = (y_ref[h, :, :D] + dot(cat([hi, lo], 1), cat([z, z], 0))).astype(bf16)


def leave(parts, y, z):
    n = sum(x[0].shape[0] for x in parts)
    args = [x for p in parts for x in p] + [y, z]
    return pl.pallas_call(
        leave_body, in_specs=[VMEM] * len(args), out_specs=VMEM, out_shape=jax.ShapeDtypeStruct((n + D, y.shape[0] * D), bf16),
        cost_estimate=cost(0.5), name="leave", compiler_params=params(8))(*args)


def weigh_body(q_ref, kp_ref, ko_ref, p_ref, *, axis, R, first):
    n = q_ref.shape[0]
    h = pl.program_id(0)
    bias = jnp.where(lax.axis_index(axis) > 0, 0.0, -1e30).astype(f32)
    scale = D ** -0.5 * math.log2(math.e)
    tri = lax.broadcasted_iota(jnp.int32, (R, R), 1) <= lax.broadcasted_iota(jnp.int32, (R, R), 0)
    kp = kp_ref[:, pl.ds(pl.multiple_of((first + h) * D, D), D)]
    for i in range(n // R):
        q = q_ref[i * R:(i + 1) * R]
        sp = dot_nt(q, kp) + bias
        so = dot_nt(q, ko_ref[:(i + 1) * R])
        diag = jnp.where(tri, so[:, i * R:], -1e30)
        so = diag if i == 0 else cat([so[:, :i * R], diag], 1)
        m = jnp.maximum(jnp.max(sp, 1, keepdims=True), jnp.max(so, 1, keepdims=True))
        ep = jnp.exp2((sp - m) * scale)
        eo = jnp.exp2((so - m) * scale)
        inv = 1.0 / (jnp.sum(ep, 1, keepdims=True) + jnp.sum(eo, 1, keepdims=True))
        p_ref[0, i * R:(i + 1) * R, :n] = (ep * inv).astype(bf16)
        p_ref[0, i * R:(i + 1) * R, n:n + (i + 1) * R] = (eo * inv).astype(bf16)
        if (i + 1) * R < n:
            p_ref[0, i * R:(i + 1) * R, n + (i + 1) * R:] = jnp.zeros((R, n - (i + 1) * R), bf16)


def weigh(q, kp, ko, g, HB, R=256, axis="ctx"):
    n, w = q.shape
    flat = pl.BlockSpec((n, D), lambda h: (0, g * HB + h))
    return pl.pallas_call(
        functools.partial(weigh_body, axis=axis, R=R, first=g * HB), grid=(HB,),
        in_specs=[flat, VMEM, flat], out_specs=pl.BlockSpec((1, n, 2 * n), lambda h: (h, 0, 0)),
        out_shape=jax.ShapeDtypeStruct((HB, n, 2 * n), bf16),
        cost_estimate=cost(HB * 1.3), name="weigh", compiler_params=params(24))(q, kp, ko)


def gather_body(*refs, step, count):
    parts, (p_ref, vz_ref) = refs[:2 * count], refs[2 * count:2 * count + 2]
    ret_ref, out_ref = refs[-2:]
    n = ret_ref.shape[0]
    for h in range(step):
        s = slice(h * D, h * D + D)
        vz = vz_ref[:, pl.ds(pl.multiple_of((pl.program_id(0) * step + h) * D, D), D)]
        mine = pl.ds(pl.multiple_of((pl.program_id(0) * step + h) * D, D), D)
        ret = cat([(o[:, mine] + dot(qe[:, mine], vz[n:])).astype(bf16) for o, qe in zip(parts[::2], parts[1::2])], 0)
        ret_ref[:, s] = ret
        out_ref[:, s] = dot(p_ref[pl.program_id(0) * step + h], cat([vz[:n], ret], 0)).astype(bf16)


def gather(parts, p, vz, carry, g, HB, w):
    n = p.shape[1]
    step = math.gcd(STEP, HB)
    args = [x for pair in parts for x in pair]
    flat = pl.BlockSpec((n, step * D), lambda h: (0, g * (HB // step) + h))
    held = [pl.BlockSpec(memory_space=pl.ANY)] * len(carry)
    return pl.pallas_call(
        functools.partial(gather_body, step=step, count=len(parts)), grid=(HB // step,),
        in_specs=[VMEM] * (len(args) + 2) + held,
        out_specs=[flat, flat], out_shape=[jax.ShapeDtypeStruct((n, w), bf16)] * 2,
        input_output_aliases={len(args) + 2 + i: i for i in range(len(carry))},
        cost_estimate=cost(HB * 0.5), name="gather", compiler_params=params(24))(*args, p, vz, *carry)


def send(array, pairs):
    return lax.ppermute(array, "ctx", pairs) if pairs else jnp.zeros_like(array)


def per_device(queries, keys, values, betas, log_decay, attn_queries, attn_keys):
    n, w = queries.shape
    HB = w // D // 2
    chunks = n // 64
    blocks = lax.axis_size("ctx")
    every = [(i, i + 1) for i in range(blocks - 1)]
    keys_behind = send(attn_keys, every)

    def pass_on(parts, y, near, far):
        z = meet(near, far)
        for k in range(3, blocks - 1):
            z = z + send(hop(y, z), [(k - 1, k)])
        return leave(parts, y, z)

    def round_one(am, a):
        far = send(a, [(0, 2)] if blocks > 2 else [])
        return send(am, every[:2]), far

    small = cat([betas[:, 0], betas[:, 1], log_decay], 1).transpose(1, 0)
    o0, qe0, rows, q1, k1, v1, y0, am, a = local_open(queries, keys, values, small, HB)
    near, far = round_one(am, a)
    first = ((o0, qe0),)
    oa, qa, y1 = local_half(q1, k1, v1, rows, HB, 0, chunks // 2)
    near, far, y1 = lax.optimization_barrier((near, far, y1))
    leaving = pass_on(first, y0, near, far)
    leaving, y1 = lax.optimization_barrier((leaving, y1))
    crossing0 = send(leaving, every)
    ob, qb, y1, am, a = local_half(q1, k1, v1, rows, HB, chunks // 2, chunks, y1)
    second = ((oa, qa), (ob, qb))
    near, far = round_one(am, a)
    keys_behind, y1 = lax.optimization_barrier((keys_behind, y1))
    weights = [weigh(attn_queries, keys_behind, attn_keys, 0, HB)]
    keys_behind, crossing0, weights = lax.optimization_barrier((keys_behind, crossing0, weights))
    weights.append(weigh(attn_queries, keys_behind, attn_keys, 1, HB))
    near, far, weights = lax.optimization_barrier((near, far, weights))
    crossing1 = send(pass_on(second, y1, near, far), every)
    done = gather(first, weights[0], crossing0, (), 0, HB, w)
    return tuple(gather(second, weights[1], crossing1, tuple(done), 1, HB, w))


def solution(mesh):
    rows, cols = ("groups", "ctx"), ("head", "sub")
    flat, paired = P(rows, cols), P(rows, None, cols)
    return jax.shard_map(
        per_device,
        mesh=mesh,
        in_specs=(flat, paired, paired, paired, flat, flat, flat),
        out_specs=(flat, flat),
        check_vma=False,
    )
```
